128 devices in a mesh: dom: 128 (over y, x, z, core).
Axes of the slice: x: 4, y: 4, z: 4, core: 2. Of those that a mesh axis runs over, the one named last changes fastest.
Arguments:
- vectors: bfloat16 [64, 524288], P(None, 'dom')
- diag_tiles: bfloat16 [4096, 128, 128], P('dom'), as said below
- pair_tiles: bfloat16 [12288, 2, 128, 128], P('dom'), as said below
- halo_tiles: bfloat16 [16384, 128, 128], P('dom'), as said below
- halo_rows: int32 [128, 128], P('dom'), may hold values from 1 to 31, as said below
- pair_index: int32 [128, 96, 2], P('dom'), may hold values from 0 to 31, as said below
- pair_count: int32 [128], P('dom'), may hold values from 24 to 96, as said below
Outputs:
- basis: bfloat16 [64, 524288], P(None, 'dom')
- ritz: float32 [64, 64], replicated
The draws below stay inside these ranges and needn't reach their ends.
Inputs may be any that keep to these rules, and one draw needn't show every extreme that they name: `diag_tiles`: each tile is symmetric. `pair_tiles`: entry [j, 1] is the transpose of entry [j, 0]. `halo_tiles`: entry d * 128 + p is the transpose of entry p * 128 + d. `halo_rows`: no entry is a multiple of 4. `pair_index`: the 96 entries of a partition are distinct pairs (r, c) with r < c. The first pair_count[d] entries of pair_index[d] are live; some partition has 96.
All inputs are finite; a program needn't handle non-finite values.
Results may differ from the reference program's by a relative error of at most 0.023.
Values may be sent and summed in bfloat16 or wider, within the bound.
No kernel may reach another device: no remote copies, remote signals or barrier semaphores. Data moves between devices by JAX's collectives and lax.ppermute only.
A program may use at most 128 MiB of HBM per device.

```python
import math
import jax
import jax.numpy as jnp
import numpy as np
from jax import lax

K = 64
B = 128
BD = 32
DEGREE = 4
EMAX = 96
PEERS = 128
ROWS = 524288


def tile_scale():
    return 0.5 / math.sqrt(B * (1.0 + 1.2 * EMAX / BD + PEERS / BD))


def tile_noise(key, shape):
    return jax.random.normal(key, shape, jnp.float32)


def draw_vectors(key, part):
    key_base = jax.random.fold_in(jax.random.fold_in(key, 11), 0)
    key_mix = jax.random.fold_in(jax.random.fold_in(key, 11), 1)
    key_common = jax.random.fold_in(jax.random.fold_in(key, 11), 3)
    normal_draw = jax.random.normal(key_base, (K, ROWS), jnp.float32)
    common_row = jax.random.normal(key_common, (1, ROWS), jnp.float32)
    normal_draw = normal_draw + 2.5 * common_row
    mixing = jnp.eye(K, dtype=jnp.float32) + 0.3 * jax.random.normal(key_mix, (K, K), jnp.float32) / math.sqrt(K)
    return jnp.dot(mixing, normal_draw).astype(jnp.bfloat16)


def draw_diag_tiles(key, part):
    normal_draw = tile_noise(jax.random.fold_in(key, 21), (PEERS * BD, B, B))
    symmetric = (normal_draw + jnp.swapaxes(normal_draw, 1, 2)) * (tile_scale() / math.sqrt(2.0))
    position = (jnp.arange(PEERS * BD) // BD).astype(jnp.float32) / max(PEERS - 1, 1)
    block_place = jnp.arange(PEERS * BD) % BD
    rough = jax.random.uniform(jax.random.fold_in(key, 22), (PEERS * BD,), jnp.float32, 0.0, 1.0)
    upper_shift = 0.3 + 0.3 * rough + 0.2 * position
    shift = jnp.where(block_place % 4 == 0, 0.05, upper_shift)
    symmetric = symmetric + shift[:, None, None] * jnp.eye(B, dtype=jnp.float32)[None, :, :]
    return symmetric.astype(jnp.bfloat16)


def draw_pair_tiles(key, part):
    normal_draw = tile_noise(jax.random.fold_in(key, 31), (PEERS * EMAX, B, B)) * tile_scale()
    return jnp.stack([normal_draw, jnp.swapaxes(normal_draw, 1, 2)], axis=1).astype(jnp.bfloat16)


def draw_halo_tiles(key, part):
    normal_draw = tile_noise(jax.random.fold_in(key, 41), (PEERS, PEERS, B, B)) * tile_scale()
    mirrored = jnp.swapaxes(jnp.swapaxes(normal_draw, 0, 1), 2, 3)
    own_ids = jnp.arange(PEERS)[:, None, None, None]
    peer_ids = jnp.arange(PEERS)[None, :, None, None]
    symmetric = jnp.where(own_ids < peer_ids, normal_draw, jnp.where(own_ids > peer_ids, mirrored, (normal_draw + mirrored) / math.sqrt(2.0)))
    return symmetric.reshape(PEERS * PEERS, B, B).astype(jnp.bfloat16)


def draw_halo_rows(key, part):
    key_group, key_offset, key_spot = jax.random.split(jax.random.fold_in(key, 71), 3)
    groups = jax.random.randint(key_group, (PEERS * PEERS,), 0, BD // 4)
    offsets = jax.random.randint(key_offset, (PEERS * PEERS,), 1, 4)
    values = 4 * groups + offsets
    spot = jax.random.randint(key_spot, (), 0, PEERS * PEERS)
    flat_iota = jnp.arange(PEERS * PEERS)
    values = jnp.where(flat_iota == spot, 1, values)
    values = jnp.where(flat_iota == (spot + 1) % (PEERS * PEERS), BD - 1, values)
    return values.reshape(PEERS, PEERS).astype(jnp.int32)


def draw_pair_index(key, part):
    first_rows, second_cols = np.triu_indices(BD, 1)
    pair_total = BD * (BD - 1) // 2
    scores = jax.random.randint(jax.random.fold_in(key, 51), (PEERS, pair_total), 0, 1 << 16) * pair_total + jnp.arange(pair_total)[None, :]
    chosen = jnp.argsort(scores, axis=1)[:, :EMAX]
    row_ids = jnp.asarray(first_rows, jnp.int32)[chosen]
    col_ids = jnp.asarray(second_cols, jnp.int32)[chosen]
    return jnp.stack([row_ids, col_ids], axis=-1).astype(jnp.int32)


def draw_pair_count(key, part):
    key_level, key_busy = jax.random.split(jax.random.fold_in(key, 61))
    levels = jax.random.randint(key_level, (PEERS,), 0, 3)
    counts = EMAX // jnp.left_shift(jnp.ones((PEERS,), jnp.int32), levels)
    busiest = jax.random.randint(key_busy, (), 0, PEERS)
    return jnp.where(jnp.arange(PEERS) == busiest, EMAX, counts).astype(jnp.int32)


def setup_inputs(seed: int = 0) -> dict:
    seeds = jax.random.split(jax.random.key(seed), 8)
    return {
        "vectors": draw_vectors(jax.random.fold_in(seeds[7], 71), 0),
        "diag_tiles": draw_diag_tiles(jax.random.fold_in(seeds[7], 71), 0),
        "pair_tiles": draw_pair_tiles(jax.random.fold_in(seeds[7], 71), 0),
        "halo_tiles": draw_halo_tiles(jax.random.fold_in(seeds[7], 71), 0),
        "halo_rows": draw_halo_rows(jax.random.fold_in(seeds[7], 71), 0),
        "pair_index": draw_pair_index(jax.random.fold_in(seeds[7], 71), 0),
        "pair_count": draw_pair_count(jax.random.fold_in(seeds[7], 71), 0),
    }


first_centre = -0.5

def apply_matrix(current, diag_tiles, pair_tiles, halo_tiles, halo_rows, pair_index, pair_count):
    blocked = current.astype(jnp.float32).reshape(K, PEERS, BD, B)
    diag_all = diag_tiles.reshape(PEERS, BD, B, B)
    pair_all = pair_tiles.reshape(PEERS, EMAX, 2, B, B)
    halo_all = halo_tiles.reshape(PEERS, PEERS, B, B)
    block_iota = jnp.arange(BD)

    def device_terms(device):
        own = blocked[:, device]
        result = jnp.einsum('krj,rij->kri', own, diag_all[device].astype(jnp.float32))
        row_ids = pair_index[device, :, 0]
        col_ids = pair_index[device, :, 1]
        live_mask = (jnp.arange(EMAX) < pair_count[device]).astype(jnp.float32)
        tiles_here = pair_all[device].astype(jnp.float32)
        upper_terms = jnp.einsum('kej,eij->kei', own[:, col_ids], tiles_here[:, 0])
        lower_terms = jnp.einsum('kej,eij->kei', own[:, row_ids], tiles_here[:, 1])
        onehot_first = (row_ids[:, None] == block_iota[None, :]).astype(jnp.float32) * live_mask[:, None]
        onehot_second = (col_ids[:, None] == block_iota[None, :]).astype(jnp.float32) * live_mask[:, None]
        result = result + jnp.einsum('kei,er->kri', upper_terms, onehot_first)
        result = result + jnp.einsum('kei,er->kri', lower_terms, onehot_second)
        sources = blocked[:, jnp.arange(PEERS), halo_rows[:, device]]
        products = jnp.einsum('kpj,pij->kpi', sources, halo_all[device].astype(jnp.float32))
        onehot_halo = (halo_rows[device][:, None] == block_iota[None, :]).astype(jnp.float32)
        return result + jnp.einsum('kpi,pr->kri', products, onehot_halo)
    stacked = lax.map(device_terms, jnp.arange(PEERS))
    return jnp.transpose(stacked, (1, 0, 2, 3)).reshape(K, ROWS)

def subspace_step(start, first, centre, operator):
    previous = start
    current = (first - centre * start.astype(jnp.float32)).astype(jnp.bfloat16)
    for degree in range(DEGREE - 1):
        applied = operator(current)
        following = (2.0 * (applied - centre * current.astype(jnp.float32)) - previous.astype(jnp.float32)).astype(jnp.bfloat16)
        previous, current = (current, following)
    gram_matrix = jnp.dot(current.astype(jnp.float32), current.T.astype(jnp.float32), preferred_element_type=jnp.float32) / ROWS
    chol_lower = jnp.linalg.cholesky(gram_matrix)
    inverse = jax.scipy.linalg.solve_triangular(chol_lower, jnp.eye(K, dtype=jnp.float32), lower=True)
    following = jnp.dot(inverse, current.astype(jnp.float32), precision=lax.Precision.HIGHEST).astype(jnp.bfloat16)
    applied = operator(following)
    projected = jnp.dot(following.astype(jnp.float32), applied.T, precision=lax.Precision.HIGHEST) / ROWS
    return (following, applied, projected)

def reference(vectors, diag_tiles, pair_tiles, halo_tiles, halo_rows, pair_index, pair_count):

    def operator(current):
        return apply_matrix(current, diag_tiles, pair_tiles, halo_tiles, halo_rows, pair_index, pair_count)
    first = operator(vectors)
    basis_one, image_one, projected_one = subspace_step(vectors, first, first_centre, operator)
    centre_two = jnp.trace(projected_one) / K - 1.0
    basis, image_two, ritz = subspace_step(basis_one, image_one, centre_two, operator)
    return (basis, ritz)
```

```python
import functools

import jax
import jax.numpy as jnp
from jax import lax
from jax.experimental import pallas as pl
from jax.experimental.pallas import tpu as pltpu
from jax.sharding import PartitionSpec as P

FIRST_CENTRE = -0.5
F32, BF16 = jnp.float32, jnp.bfloat16
HI = lax.Precision.HIGHEST
VM = pl.BlockSpec(memory_space=pltpu.VMEM)
SM = pl.BlockSpec(memory_space=pltpu.SMEM)
UNROLL = 8


def held(x):
    return pltpu.with_memory_space_constraint(x, pltpu.VMEM)


def call(body, outs, ins, flops, moved, scratch=()):
    return pl.pallas_call(
        body,
        out_shape=[pltpu.VMEM(s, d) for s, d in outs],
        in_specs=[SM if kind == "s" else VM for _, kind in ins],
        out_specs=[VM for _ in outs],
        scratch_shapes=list(scratch),
        cost_estimate=pl.CostEstimate(flops=flops, bytes_accessed=moved, transcendentals=0),
        compiler_params=pltpu.CompilerParams(vmem_limit_bytes=30 << 20),
    )(*[held(x) if kind == "v" else x for x, kind in ins])


def mm(a, b):
    return jnp.dot(a, b, preferred_element_type=F32)


def mm_t(a, b, precision=None):
    return lax.dot_general(a, b, (((1,), (1,)), ((), ())), precision=precision, preferred_element_type=F32)


def spread(rows_ref, blocks_ref, out_ref):
    peers = out_ref.shape[0]

    def step(i, _):
        for u in range(UNROLL):
            p = i * UNROLL + u
            out_ref[p] = blocks_ref[rows_ref[p]]
        return _

    lax.fori_loop(0, peers // UNROLL, step, 0)


def start_kernel(rows_ref, vec_ref, cur_ref, out_ref):
    width = cur_ref.shape[2]
    for r in range(cur_ref.shape[0]):
        cur_ref[r] = vec_ref[:, r * width : (r + 1) * width]
    spread(rows_ref, cur_ref, out_ref)


def tile_kernel(tiles_ref, out_ref):
    def step(i, _):
        for u in range(4):
            out_ref[i * 4 + u] = tiles_ref[i * 4 + u].T
        return _

    lax.fori_loop(0, out_ref.shape[0] // 4, step, 0)


def pair_sums(first_ref, second_ref, count_ref, cur_ref, pair_ref, acc_ref):
    count = count_ref[0]
    group = 4

    def step(i, _):
        parts = []
        for u in range(group):
            e = i * group + u
            live = jnp.where(e < count, 1.0, 0.0).astype(F32)
            r, c = first_ref[e], second_ref[e]
            parts.append((r, mm(cur_ref[c], pair_ref[e, 1]) * live))
            parts.append((c, mm(cur_ref[r], pair_ref[e, 0]) * live))
        for at, value in parts:
            acc_ref[at] += value
        return _

    lax.fori_loop(0, lax.div(count + (group - 1), group), step, 0)


def local_kernel(mode, total, first_ref, second_ref, count_ref, *refs):
    if mode == "second":
        cur_ref, diag_ref, pair_ref, image_ref, prev_ref, trace_ref, acc_ref, y_ref, c_ref = refs
        centre = jnp.sum(trace_ref[...]) / (total * prev_ref.shape[1]) - 1.0
        c_ref[...] = jnp.full(c_ref.shape, centre, F32)
    elif mode == "filter":
        centre_ref, cur_ref, diag_ref, pair_ref, prev_ref, acc_ref = refs
        centre = centre_ref[0, 0]
    else:
        cur_ref, diag_ref, pair_ref, acc_ref = refs
        centre = FIRST_CENTRE

    def own(r, _):
        block = cur_ref[r]
        value = mm(block, diag_ref[r])
        if mode == "start":
            value = value - centre * block.astype(F32)
        if mode == "filter":
            value = value - centre * block.astype(F32) - 0.5 * prev_ref[r].astype(F32)
        if mode == "second":
            image, prev = image_ref[r], prev_ref[r].astype(F32)
            y = (image - centre * prev).astype(BF16)
            y_ref[r] = y
            value = value - centre * (image + y.astype(F32)) - 0.5 * prev
        acc_ref[r] = value
        return _

    lax.fori_loop(0, cur_ref.shape[0], own, 0, unroll=4)
    pair_sums(first_ref, second_ref, count_ref, cur_ref, pair_ref, acc_ref)


def halo_sums(rows_ref, arrived_ref, tiles_ref, acc_ref):
    def step(i, _):
        parts = []
        for u in range(UNROLL):
            p = i * UNROLL + u
            parts.append((rows_ref[p], mm(arrived_ref[p], tiles_ref[p])))
        for at, value in parts:
            acc_ref[at] += value
        return _

    lax.fori_loop(0, arrived_ref.shape[0] // UNROLL, step, 0)


def halo_kernel(mode, rows_ref, arrived_ref, tiles_ref, part_ref, *refs):
    acc_ref = refs[-1]
    acc_ref[...] = part_ref[...]
    halo_sums(rows_ref, arrived_ref, tiles_ref, acc_ref)
    blocks = acc_ref.shape[0]
    if mode == "image":
        inverse_ref, image_ref, cur_ref, out_ref, _ = refs
        for r in range(blocks):
            image = jnp.dot(inverse_ref[...], acc_ref[r], precision=HI, preferred_element_type=F32)
            image_ref[r] = image
            cur_ref[r] = image.astype(BF16)
        spread(rows_ref, cur_ref, out_ref)
    elif mode == "last":
        filtered_ref, sum_ref, _ = refs
        value = jnp.zeros(sum_ref.shape, F32)
        for r in range(blocks):
            value = value + mm_t(filtered_ref[r].astype(F32), acc_ref[r], HI)
        sum_ref[...] = value
    else:
        cur_ref, out_ref, _ = refs
        factor = 1.0 if mode == "start" else 2.0
        cur_ref[...] = (factor * acc_ref[...]).astype(BF16)
        spread(rows_ref, cur_ref, out_ref)


def gram_kernel(total, cur_ref, gram_ref):
    value = jnp.zeros(gram_ref.shape, F32)
    for r in range(cur_ref.shape[0]):
        block = cur_ref[r]
        value = value + mm_t(block, block)
    gram_ref[...] = value / total


def factor_kernel(flat, gram_ref, cur_ref, inverse_ref, next_ref):
    n = gram_ref.shape[0]
    row = lax.broadcasted_iota(jnp.int32, (n, n), 0)
    col = lax.broadcasted_iota(jnp.int32, (n, n), 1)
    work = jnp.concatenate([gram_ref[...], jnp.where(row == col, 1.0, 0.0).astype(F32)], axis=1)
    at = lax.broadcasted_iota(jnp.int32, (n, 1), 0)
    for j in range(n - 1):
        times = jnp.where(at > j, work[:, j : j + 1] / work[j : j + 1, j : j + 1], 0.0)
        work = work - times * work[j : j + 1, :]
    pivots = jnp.sum(jnp.where(row == col, work[:, :n], 0.0), axis=1, keepdims=True)
    inverse = work[:, n:] / jnp.sqrt(pivots)
    inverse_ref[...] = inverse
    width = cur_ref.shape[2]
    for r in range(cur_ref.shape[0]):
        block = jnp.dot(inverse, cur_ref[r].astype(F32), precision=HI, preferred_element_type=F32).astype(BF16)
        if flat:
            next_ref[:, r * width : (r + 1) * width] = block
        else:
            next_ref[r] = block


def trace_kernel(image_ref, next_ref, out_ref):
    value = jnp.zeros(image_ref.shape[1:], F32)
    for r in range(image_ref.shape[0]):
        value = value + image_ref[r] * next_ref[r].astype(F32)
    out_ref[...] = jnp.sum(value.reshape(-1, 8, value.shape[1]), axis=0)


def ritz_kernel(total, inverse_ref, sum_ref, ritz_ref):
    inverse = inverse_ref[...]
    half = jnp.dot(inverse, sum_ref[...], precision=HI, preferred_element_type=F32)
    ritz_ref[...] = mm_t(half, inverse, HI) / total


def everywhere(x, devices):
    step = 1
    while step < devices:
        x = x + lax.ppermute(x, "dom", [(i, i ^ step) for i in range(devices)])
        step *= 2
    return x


def local(vectors, diag_tiles, pair_tiles, halo_tiles, halo_rows, pair_index, pair_count):
    k, own_rows = vectors.shape
    blocks, size, _ = diag_tiles.shape
    edges, peers = pair_index.shape[1], halo_rows.shape[1]
    total = float(own_rows * peers)
    rows = halo_rows[0]
    index = ((pair_index[0, :, 0], "s"), (pair_index[0, :, 1], "s"), (pair_count, "s"))
    block = ((blocks, k, size), BF16)
    wide = ((blocks, k, size), F32)
    spots = ((peers, k, size), BF16)
    square = ((k, k), F32)
    unit = 2 * k * size * size

    [tiles] = call(tile_kernel, [((peers, size, size), BF16)], [(halo_tiles, "v")], 1 << 20, 8 << 20)

    def exchange(out):
        return lax.all_to_all(out, "dom", 0, 0, tiled=True)

    def own(mode, cur, extra=(), ahead=(), outs=()):
        ins = [*index, *ahead, (cur, "v"), (diag_tiles, "v"), (pair_tiles.reshape(edges, 2, size, size), "v"), *extra]
        return call(functools.partial(local_kernel, mode, total), [wide, *outs], ins, unit * (blocks + 2 * edges), 9 << 20)

    def halo(mode, arrived, part, outs, extra=()):
        ins = [(rows, "s"), (arrived, "v"), (tiles, "v"), (part, "v"), *extra]
        scratch = [pltpu.VMEM((blocks, k, size), F32)]
        return call(functools.partial(halo_kernel, mode), outs, ins, unit * peers, 10 << 20, scratch)

    def gram(cur):
        [value] = call(functools.partial(gram_kernel, total), [square], [(cur, "v")], 2 * k * k * own_rows, 1 << 20)
        return everywhere(value, peers)

    def factor(total_gram, cur, flat):
        outs = [square, ((k, own_rows), BF16) if flat else block]
        return call(functools.partial(factor_kernel, flat), outs, [(total_gram, "v"), (cur, "v")], 1 << 24, 2 << 20)

    def filtered(prev, cur, out, centre, steps):
        for _ in range(steps):
            arrived = exchange(out)
            [part] = own("filter", cur, [(prev, "v")], [(centre, "s")])
            prev, (cur, out) = cur, halo("filter", arrived, part, [block, spots])
        return cur, out

    start, out = call(start_kernel, [block, spots], [(rows, "s"), (vectors, "v")], 1 << 20, 4 << 20)
    arrived = exchange(out)
    [part] = own("start", start)
    cur, out = halo("start", arrived, part, [block, spots])
    cur, out = filtered(start, cur, out, jnp.full((1, 1), FIRST_CENTRE, F32), 3)

    arrived = exchange(out)
    inverse, basis_one = factor(gram(cur), cur, False)
    [part] = own("image", cur)
    image, cur, out = halo("image", arrived, part, [wide, block, spots], [(inverse, "v")])

    arrived = exchange(out)
    [trace] = call(trace_kernel, [((8, size), F32)], [(image, "v"), (basis_one, "v")], 1 << 20, 2 << 20)
    extra = [(image, "v"), (basis_one, "v"), (everywhere(trace, peers), "v")]
    part, first, centre = own("second", cur, extra, (), [block, ((8, size), F32)])
    cur, out = halo("filter", arrived, part, [block, spots])
    cur, out = filtered(first, cur, out, centre, 2)

    arrived = exchange(out)
    inverse, basis = factor(gram(cur), cur, True)
    [part] = own("image", cur)
    [partial] = halo("last", arrived, part, [square], [(cur, "v")])
    [ritz] = call(
        functools.partial(ritz_kernel, total), [square], [(inverse, "v"), (everywhere(partial, peers), "v")], 1 << 20, 1 << 16
    )
    return basis, ritz


def solution(mesh):
    return jax.shard_map(
        local,
        mesh=mesh,
        in_specs=(
            P(None, "dom"),
            P("dom", None, None),
            P("dom", None, None, None),
            P("dom", None, None),
            P("dom", None),
            P("dom", None, None),
            P("dom"),
        ),
        out_specs=(P(None, "dom"), P()),
        check_vma=False,
    )
```

```python
import functools

import jax
import jax.numpy as jnp
from jax import lax
from jax.experimental import pallas as pl
from jax.experimental.pallas import tpu as pltpu
from jax.sharding import PartitionSpec as P

FIRST_CENTRE = -0.5
F32, BF16 = jnp.float32, jnp.bfloat16
HI = lax.Precision.HIGHEST
VM = pl.BlockSpec(memory_space=pltpu.VMEM)
SM = pl.BlockSpec(memory_space=pltpu.SMEM)


HBM = pl.BlockSpec(memory_space=pltpu.HBM)
NODE = 8


def call(body, outs, ins, flops, moved, scratch=()):
    place = {"a": pltpu.HBM, "v": pltpu.VMEM}
    spec = {"a": HBM, "v": VM, "h": VM, "s": SM}
    return pl.pallas_call(
        body,
        out_shape=[(place[kind] if kind in place else jax.ShapeDtypeStruct)(shape, dtype) for shape, dtype, kind in outs],
        in_specs=[spec[kind] for _, kind in ins],
        out_specs=[spec[kind] for _, _, kind in outs],
        scratch_shapes=list(scratch),
        cost_estimate=pl.CostEstimate(flops=flops, bytes_accessed=moved, transcendentals=0),
        compiler_params=pltpu.CompilerParams(vmem_limit_bytes=30 << 20),
    )(*[pltpu.with_memory_space_constraint(x, place[kind]) if kind in place else x for x, kind in ins])


def mm(a, b):
    return jnp.dot(a, b, preferred_element_type=F32)


def mm_t(a, b, precision=None):
    return lax.dot_general(a, b, (((1,), (1,)), ((), ())), precision=precision, preferred_element_type=F32)


def thirds(x):
    high = x.astype(BF16)
    rest = x - high.astype(F32)
    middle = rest.astype(BF16)
    return high, middle, (rest - middle.astype(F32)).astype(BF16)


def begin(source, target, sem):
    copy = pltpu.make_async_copy(source, target, sem)
    copy.start()
    return copy


def spread(rows_ref, blocks_ref, slots_ref, out_ref, sems):
    half = slots_ref.shape[0] // 2
    copies = []
    for g in range(2):
        for p in range(g * half, (g + 1) * half):
            slots_ref[p] = blocks_ref[rows_ref[p]]
        copies.append(begin(slots_ref.at[pl.ds(g * half, half)], out_ref.at[pl.ds(g * half, half)], sems.at[g]))
    return copies


def start_kernel(rows_ref, vec_ref, cur_ref, out_ref, slots, sems):
    width = cur_ref.shape[2]
    for r in range(cur_ref.shape[0]):
        cur_ref[r] = vec_ref[:, r * width : (r + 1) * width]
    for copy in spread(rows_ref, cur_ref, slots, out_ref, sems):
        copy.wait()


def tile_kernel(tiles_ref, out_ref):
    def step(i, _):
        for u in range(4):
            out_ref[i * 4 + u] = tiles_ref[i * 4 + u].T
        return _

    lax.fori_loop(0, out_ref.shape[0] // 4, step, 0)


def local_kernel(mode, first_ref, second_ref, count_ref, *refs):
    if mode == "filter":
        centre_ref, cur_ref, diag_ref, pair_ref, prev_ref, acc_ref = refs
        centre = centre_ref[0, 0]
    else:
        cur_ref, diag_ref, pair_ref, acc_ref = refs
        centre = FIRST_CENTRE

    def own(r, _):
        block = cur_ref[r]
        value = mm(block, diag_ref[r])
        if mode != "image":
            value = value - centre * block.astype(F32)
        if mode == "filter":
            value = value - 0.5 * prev_ref[r].astype(F32)
        acc_ref[r] = value
        return _

    lax.fori_loop(0, cur_ref.shape[0], own, 0, unroll=4)
    count = count_ref[0]
    group = 4

    def step(i, _):
        parts = []
        for u in range(group):
            e = i * group + u
            live = jnp.where(e < count, 1.0, 0.0).astype(F32)
            r, c = first_ref[e], second_ref[e]
            parts.append((r, mm(cur_ref[c], pair_ref[e, 1]) * live))
            parts.append((c, mm(cur_ref[r], pair_ref[e, 0]) * live))
        for at, value in parts:
            acc_ref[at] += value
        return _

    lax.fori_loop(0, lax.div(count + (group - 1), group), step, 0)


def halo_sums(rows_ref, arrived_ref, tiles_ref, acc_ref):
    parts = []
    for p in range(arrived_ref.shape[0]):
        parts.append((rows_ref[p], mm(arrived_ref[p], tiles_ref[p])))
        if len(parts) > 8:
            at, value = parts.pop(0)
            acc_ref[at] += value
    for at, value in parts:
        acc_ref[at] += value


def halo_kernel(factor, rows_ref, arrived_ref, tiles_ref, part_ref, cur_ref, out_ref, tiles, part, acc, block, slots, sems):
    coming = begin(tiles_ref, tiles, sems.at[0])
    also = begin(part_ref, part, sems.at[1])
    acc[...] = jnp.zeros(acc.shape, F32)
    coming.wait()
    halo_sums(rows_ref, arrived_ref, tiles, acc)
    also.wait()
    block[...] = (factor * (acc[...] + part[...])).astype(BF16)
    going = [begin(block, cur_ref, sems.at[2])]
    going += spread(rows_ref, block, slots, out_ref, sems)
    for copy in going:
        copy.wait()


def gram_kernel(cur_ref, gram_ref):
    value = jnp.zeros(gram_ref.shape, F32)
    for r in range(cur_ref.shape[0]):
        block = cur_ref[r]
        value = value + mm_t(block, block)
    gram_ref[...] = value


def sums_kernel(keep, rows_ref, arrived_ref, tiles_ref, part_ref, cur_ref, gram_ref, *refs):
    if keep:
        image_ref, sums_ref, tiles, acc, halo, cur, sems = refs
    else:
        sums_ref, tiles, acc, halo, cur, sems = refs
    coming = begin(tiles_ref, tiles, sems.at[0])
    also = begin(part_ref, acc, sems.at[1])
    more = begin(cur_ref, cur, sems.at[2])
    halo[...] = jnp.zeros(halo.shape, F32)
    coming.wait()
    halo_sums(rows_ref, arrived_ref, tiles, halo)
    also.wait()
    acc[...] += halo[...]
    if keep:
        going = begin(acc, image_ref, sems.at[0])
    more.wait()
    k = gram_ref.shape[0]
    value = jnp.zeros((k, k), F32)
    for r in range(acc.shape[0]):
        block = cur[r]
        for third in thirds(acc[r]):
            value = value + mm_t(block, third)
    sums_ref[...] = jnp.concatenate([gram_ref[...], value], axis=1)
    if keep:
        going.wait()


def inverse_factor(gram):
    n = gram.shape[0]
    row = lax.broadcasted_iota(jnp.int32, (n, n), 0)
    col = lax.broadcasted_iota(jnp.int32, (n, n), 1)
    work = jnp.concatenate([gram, jnp.where(row == col, 1.0, 0.0).astype(F32)], axis=1)
    at = lax.broadcasted_iota(jnp.int32, work.shape, 0)
    for j in range(0, n, 2):
        first = jnp.broadcast_to(work[:, j : j + 1], work.shape)
        second = jnp.broadcast_to(work[:, j + 1 : j + 2], work.shape)
        over = 1.0 / first[j : j + 1]
        low = first[j + 1 : j + 2] * over
        upper = second[j : j + 1]
        under = 1.0 / (second[j + 1 : j + 2] - low * upper)
        below = work[j + 1 : j + 2] - low * work[j : j + 1]
        times = first * over
        again = jnp.where(at > j + 1, (second - times * upper) * under, 0.0)
        work = work - jnp.where(at > j, times, 0.0) * work[j : j + 1] - again * below
    pivots = jnp.sum(jnp.where(row == col, work[:, :n], 0.0), axis=1, keepdims=True)
    return work[:, n:] / jnp.sqrt(pivots)


def apply_square(parts, block):
    return mm(parts[0], block) + (mm(parts[1], block) + mm(parts[2], block))


def turn_kernel(total, rows_ref, sums_ref, cur_ref, image_ref, next_ref, y_ref, out_ref, centre_ref, cur, image, start, block, slots, sems):
    coming = begin(cur_ref, cur, sems.at[0])
    also = begin(image_ref, image, sems.at[1])
    k = sums_ref.shape[0]
    inverse = inverse_factor(sums_ref[:, :k] / total)
    half = jnp.dot(inverse, sums_ref[:, k:] / total, precision=HI, preferred_element_type=F32)
    centre = jnp.sum(half * inverse) / k - 1.0
    centre_ref[0, 0] = centre
    parts = thirds(inverse)
    coming.wait()
    also.wait()
    for r in range(cur.shape[0]):
        begun = apply_square(parts, cur[r]).astype(BF16)
        start[r] = begun
        turned = jnp.dot(inverse, image[r], precision=HI, preferred_element_type=F32)
        block[r] = (turned - centre * begun.astype(F32)).astype(BF16)
    going = [begin(start, next_ref, sems.at[2]), begin(block, y_ref, sems.at[3])]
    going += spread(rows_ref, block, slots, out_ref, sems)
    for copy in going:
        copy.wait()


def end_kernel(total, sums_ref, cur_ref, basis_ref, ritz_ref, cur, sems):
    coming = begin(cur_ref, cur, sems.at[0])
    k, width = sums_ref.shape[0], cur.shape[2]
    inverse = inverse_factor(sums_ref[:, :k] / total)
    half = jnp.dot(inverse, sums_ref[:, k:] / total, precision=HI, preferred_element_type=F32)
    ritz_ref[...] = mm_t(half, inverse, HI)
    parts = thirds(inverse)
    coming.wait()
    for r in range(cur.shape[0]):
        basis_ref[:, r * width : (r + 1) * width] = apply_square(parts, cur[r]).astype(BF16)


def local(vectors, diag_tiles, pair_tiles, halo_tiles, halo_rows, pair_index, pair_count):
    k, own_rows = vectors.shape
    blocks, size, _ = diag_tiles.shape
    edges, peers = pair_index.shape[1], halo_rows.shape[1]
    total = float(own_rows * peers)
    rows = halo_rows[0]
    index = ((pair_index[0, :, 0], "s"), (pair_index[0, :, 1], "s"), (pair_count, "s"))
    block, spots, square = (blocks, k, size), (peers, k, size), (k, k)
    pair_tiles = pair_tiles.reshape(edges, 2, size, size)
    unit = 2 * k * size * size

    def room(shape, dtype):
        return pltpu.VMEM(shape, dtype)

    sems = pltpu.SemaphoreType.DMA((4,))
    [tiles] = call(tile_kernel, [((peers, size, size), BF16, "h")], [(halo_tiles, "h")], 1 << 20, 8 << 20)

    def exchange(out):
        return lax.all_to_all(out, "dom", 0, 0, tiled=True)

    def own(mode, cur, extra=(), ahead=()):
        ins = [*index, *ahead, (cur, "h"), (diag_tiles, "h"), (pair_tiles, "h"), *extra]
        [part] = call(functools.partial(local_kernel, mode), [(block, F32, "h")], ins, unit * (blocks + 2 * edges), 9 << 20)
        return part

    def halo(factor, arrived, part):
        return call(
            functools.partial(halo_kernel, factor),
            [(block, BF16, "a"), (spots, BF16, "a")],
            [(rows, "s"), (arrived, "v"), (tiles, "a"), (part, "a")],
            unit * peers,
            10 << 20,
            [room(tiles.shape, BF16), room(block, F32), room(block, F32), room(block, BF16), room(spots, BF16), sems],
        )

    def everywhere(x):
        near = [list(range(g, g + NODE)) for g in range(0, peers, NODE)]
        far = [list(range(g, peers, NODE)) for g in range(NODE)]
        for groups in (near, far):
            many = jnp.broadcast_to(x[None], (len(groups[0]), *x.shape))
            x = jnp.sum(lax.all_to_all(many, "dom", 0, 0, axis_index_groups=groups, tiled=True), axis=0)
        return x

    def sums(cur, arrived, part, keep):
        [gram] = call(gram_kernel, [(square, F32, "h")], [(cur, "h")], 2 * k * k * own_rows, 1 << 20)
        outs = [(block, F32, "a")] * keep + [((k, 2 * k), F32, "h")]
        ins = [(rows, "s"), (arrived, "v"), (tiles, "a"), (part, "a"), (cur, "a"), (gram, "h")]
        scratch = [room(tiles.shape, BF16), room(block, F32), room(block, F32), room(block, BF16), sems]
        *image, value = call(functools.partial(sums_kernel, keep), outs, ins, unit * peers, 10 << 20, scratch)
        return *image, everywhere(value)

    def filtered(prev, cur, out, centre):
        for _ in range(3):
            arrived = exchange(out)
            part = own("filter", cur, [(prev, "h")], [(centre, "s")])
            prev, (cur, out) = cur, halo(2.0, arrived, part)
        return cur, out

    start, out = call(
        start_kernel,
        [(block, BF16, "h"), (spots, BF16, "a")],
        [(rows, "s"), (vectors, "h")],
        1 << 20,
        4 << 20,
        [room(spots, BF16), sems],
    )
    arrived = exchange(out)
    cur, out = halo(1.0, arrived, own("start", start))
    cur, out = filtered(start, cur, out, jnp.full((1, 1), FIRST_CENTRE, F32))

    arrived = exchange(out)
    image, value = sums(cur, arrived, own("image", cur), 1)
    begun, cur, out, centre = call(
        functools.partial(turn_kernel, total),
        [(block, BF16, "a"), (block, BF16, "a"), (spots, BF16, "a"), ((1, 1), F32, "s")],
        [(rows, "s"), (value, "h"), (cur, "a"), (image, "a")],
        1 << 24,
        4 << 20,
        [room(block, BF16), room(block, F32), room(block, BF16), room(block, BF16), room(spots, BF16), sems],
    )
    cur, out = filtered(begun, cur, out, centre)

    arrived = exchange(out)
    [value] = sums(cur, arrived, own("image", cur), 0)
    return call(
        functools.partial(end_kernel, total),
        [((k, own_rows), BF16, "h"), (square, F32, "h")],
        [(value, "h"), (cur, "a")],
        1 << 24,
        2 << 20,
        [room(block, BF16), sems],
    )


def solution(mesh):
    return jax.shard_map(
        local,
        mesh=mesh,
        in_specs=(
            P(None, "dom"),
            P("dom", None, None),
            P("dom", None, None, None),
            P("dom", None, None),
            P("dom", None),
            P("dom", None, None),
            P("dom"),
        ),
        out_specs=(P(None, "dom"), P()),
        check_vma=False,
    )
```

```python
import functools

import jax
import jax.numpy as jnp
from jax import lax
from jax.experimental import pallas as pl
from jax.experimental.pallas import tpu as pltpu
from jax.sharding import PartitionSpec as P

FIRST_CENTRE = -0.5
F32, BF16 = jnp.float32, jnp.bfloat16
HI = lax.Precision.HIGHEST
VM = pl.BlockSpec(memory_space=pltpu.VMEM)
SM = pl.BlockSpec(memory_space=pltpu.SMEM)


HBM = pl.BlockSpec(memory_space=pltpu.HBM)
NODE = 8


def call(body, outs, ins, flops, moved, scratch=()):
    place = {"a": pltpu.HBM, "v": pltpu.VMEM}
    spec = {"a": HBM, "v": VM, "h": VM, "s": SM}
    return pl.pallas_call(
        body,
        out_shape=[(place[kind] if kind in place else jax.ShapeDtypeStruct)(shape, dtype) for shape, dtype, kind in outs],
        in_specs=[spec[kind] for _, kind in ins],
        out_specs=[spec[kind] for _, _, kind in outs],
        scratch_shapes=list(scratch),
        cost_estimate=pl.CostEstimate(flops=flops, bytes_accessed=moved, transcendentals=0),
        compiler_params=pltpu.CompilerParams(vmem_limit_bytes=30 << 20),
    )(*[pltpu.with_memory_space_constraint(x, place[kind]) if kind in place else x for x, kind in ins])


def mm(a, b):
    return jnp.dot(a, b, preferred_element_type=F32)


def mm_t(a, b, precision=None):
    return lax.dot_general(a, b, (((1,), (1,)), ((), ())), precision=precision, preferred_element_type=F32)


def thirds(x):
    high = x.astype(BF16)
    rest = x - high.astype(F32)
    middle = rest.astype(BF16)
    return high, middle, (rest - middle.astype(F32)).astype(BF16)


def begin(source, target, sem):
    copy = pltpu.make_async_copy(source, target, sem)
    copy.start()
    return copy


def spread(rows_ref, blocks_ref, slots_ref, out_ref, sems):
    half = slots_ref.shape[0] // 2
    copies = []
    for g in range(2):
        for p in range(g * half, (g + 1) * half):
            slots_ref[p] = blocks_ref[rows_ref[p]]
        copies.append(begin(slots_ref.at[pl.ds(g * half, half)], out_ref.at[pl.ds(g * half, half)], sems.at[g]))
    return copies


def start_kernel(rows_ref, vec_ref, cur_ref, out_ref, slots, sems):
    width = cur_ref.shape[2]
    for r in range(cur_ref.shape[0]):
        cur_ref[r] = vec_ref[:, r * width : (r + 1) * width]
    for copy in spread(rows_ref, cur_ref, slots, out_ref, sems):
        copy.wait()


def tile_kernel(tiles_ref, out_ref):
    def step(i, _):
        for u in range(4):
            out_ref[i * 4 + u] = tiles_ref[i * 4 + u].T
        return _

    lax.fori_loop(0, out_ref.shape[0] // 4, step, 0)


def local_kernel(mode, first_ref, second_ref, count_ref, *refs):
    if mode == "filter":
        centre_ref, cur_ref, diag_ref, pair_ref, prev_ref, acc_ref = refs
        centre = centre_ref[0, 0]
    else:
        cur_ref, diag_ref, pair_ref, acc_ref = refs[0], refs[1], refs[2], refs[-1]
        centre = FIRST_CENTRE

    def own(r, _):
        block = cur_ref[r]
        value = mm(block, diag_ref[r])
        if mode != "image":
            value = value - centre * block.astype(F32)
        if mode == "filter":
            value = value - 0.5 * prev_ref[r].astype(F32)
        acc_ref[r] = value
        return _

    lax.fori_loop(0, cur_ref.shape[0], own, 0, unroll=4)
    count = count_ref[0]
    group = 4

    def step(i, _):
        parts = []
        for u in range(group):
            e = i * group + u
            live = jnp.where(e < count, 1.0, 0.0).astype(F32)
            r, c = first_ref[e], second_ref[e]
            parts.append((r, mm(cur_ref[c], pair_ref[e, 1]) * live))
            parts.append((c, mm(cur_ref[r], pair_ref[e, 0]) * live))
        for at, value in parts:
            acc_ref[at] += value
        return _

    lax.fori_loop(0, lax.div(count + (group - 1), group), step, 0)


def halo_sums(rows_ref, arrived_ref, tiles_ref, acc_ref):
    parts = []
    for p in range(arrived_ref.shape[0]):
        parts.append((rows_ref[p], mm(arrived_ref[p], tiles_ref[p])))
        if len(parts) > 8:
            at, value = parts.pop(0)
            acc_ref[at] += value
    for at, value in parts:
        acc_ref[at] += value


def halo_kernel(factor, rows_ref, arrived_ref, tiles_ref, part_ref, cur_ref, out_ref, tiles, part, acc, block, slots, sems):
    coming = begin(tiles_ref, tiles, sems.at[0])
    also = begin(part_ref, part, sems.at[1])
    acc[...] = jnp.zeros(acc.shape, F32)
    coming.wait()
    halo_sums(rows_ref, arrived_ref, tiles, acc)
    also.wait()
    block[...] = (factor * (acc[...] + part[...])).astype(BF16)
    going = [begin(block, cur_ref, sems.at[2])]
    going += spread(rows_ref, block, slots, out_ref, sems)
    for copy in going:
        copy.wait()


def gram_kernel(cur_ref, gram_ref):
    value = jnp.zeros(gram_ref.shape, F32)
    for r in range(cur_ref.shape[0]):
        block = cur_ref[r]
        value = value + mm_t(block, block)
    gram_ref[...] = value


def product_kernel(cur_ref, image_ref, sum_ref):
    value = jnp.zeros(sum_ref.shape, F32)
    for r in range(cur_ref.shape[0]):
        for third in thirds(image_ref[r]):
            value = value + mm_t(cur_ref[r], third)
    sum_ref[...] = value


def image_kernel(last, rows_ref, arrived_ref, tiles_ref, part_ref, cur_ref, gram_ref, *refs):
    del gram_ref
    if last:
        sum_ref, tiles, acc, halo, cur, sems = refs
    else:
        image_ref, z_ref, out_ref, tiles, acc, halo, cur, block, slots, sems = refs
    coming = begin(tiles_ref, tiles, sems.at[0])
    also = begin(part_ref, acc, sems.at[1])
    more = begin(cur_ref, cur, sems.at[2])
    halo[...] = jnp.zeros(halo.shape, F32)
    coming.wait()
    halo_sums(rows_ref, arrived_ref, tiles, halo)
    also.wait()
    acc[...] += halo[...]
    more.wait()
    if last:
        product_kernel(cur, acc, sum_ref)
    else:
        block[...] = (acc[...] - FIRST_CENTRE * cur[...].astype(F32)).astype(BF16)
        going = [begin(acc, image_ref, sems.at[2]), begin(block, z_ref, sems.at[3])]
        going += spread(rows_ref, block, slots, out_ref, sems)
        for copy in going:
            copy.wait()


def inverse_factor(gram):
    n = gram.shape[0]
    row = lax.broadcasted_iota(jnp.int32, (n, n), 0)
    col = lax.broadcasted_iota(jnp.int32, (n, n), 1)
    work = jnp.concatenate([gram, jnp.where(row == col, 1.0, 0.0).astype(F32)], axis=1)
    at = lax.broadcasted_iota(jnp.int32, work.shape, 0)
    for j in range(0, n, 2):
        first = jnp.broadcast_to(work[:, j : j + 1], work.shape)
        second = jnp.broadcast_to(work[:, j + 1 : j + 2], work.shape)
        over = 1.0 / first[j : j + 1]
        low = first[j + 1 : j + 2] * over
        upper = second[j : j + 1]
        under = 1.0 / (second[j + 1 : j + 2] - low * upper)
        below = work[j + 1 : j + 2] - low * work[j : j + 1]
        times = first * over
        again = jnp.where(at > j + 1, (second - times * upper) * under, 0.0)
        work = work - jnp.where(at > j, times, 0.0) * work[j : j + 1] - again * below
    pivots = jnp.sum(jnp.where(row == col, work[:, :n], 0.0), axis=1, keepdims=True)
    return work[:, n:] / jnp.sqrt(pivots)


def apply_square(parts, block):
    return mm(parts[0], block) + (mm(parts[1], block) + mm(parts[2], block))


def factor_kernel(total, flat, gram_ref, cur_ref, inverse_ref, next_ref):
    width = cur_ref.shape[2]
    inverse = inverse_factor(gram_ref[...] / total)
    inverse_ref[...] = inverse
    parts = thirds(inverse)
    for r in range(cur_ref.shape[0]):
        block = apply_square(parts, cur_ref[r]).astype(BF16)
        if flat:
            next_ref[:, r * width : (r + 1) * width] = block
        else:
            next_ref[r] = block


def turn_kernel(total, rows_ref, arrived_ref, tiles_ref, part_ref, image_ref, z_ref, cur_ref, next_ref, inverse_ref, sum_ref, *refs):
    y_ref, out_ref, centre_ref, tiles, acc, part, image, z, cur, begun, block, slots, sems, late = refs
    coming = begin(tiles_ref, tiles, sems.at[0])
    also = [
        begin(source, target, late.at[i])
        for i, (source, target) in enumerate(((part_ref, part), (image_ref, image), (z_ref, z), (cur_ref, cur), (next_ref, begun)))
    ]
    acc[...] = jnp.zeros(acc.shape, F32)
    inverse = inverse_ref[...]
    half = jnp.dot(inverse, sum_ref[...] / total, precision=HI, preferred_element_type=F32)
    centre = jnp.sum(half * inverse) / inverse.shape[0] - 1.0
    change = centre - FIRST_CENTRE
    centre_ref[0, 0] = centre
    coming.wait()
    halo_sums(rows_ref, arrived_ref, tiles, acc)
    for copy in also:
        copy.wait()
    for r in range(cur.shape[0]):
        value = acc[r] + part[r] - change * image[r] - centre * (z[r].astype(F32) - change * cur[r].astype(F32))
        turned = jnp.dot(inverse, 2.0 * value, precision=HI, preferred_element_type=F32)
        block[r] = (turned - begun[r].astype(F32)).astype(BF16)
    going = [begin(block, y_ref, sems.at[2])]
    going += spread(rows_ref, block, slots, out_ref, sems)
    for copy in going:
        copy.wait()


def first_kernel(centre_ref, z_ref, cur_ref, inverse_ref, y_ref):
    change = centre_ref[0, 0] - FIRST_CENTRE
    for r in range(cur_ref.shape[0]):
        value = z_ref[r].astype(F32) - change * cur_ref[r].astype(F32)
        y_ref[r] = jnp.dot(inverse_ref[...], value, precision=HI, preferred_element_type=F32).astype(BF16)


def ritz_kernel(total, inverse_ref, sum_ref, ritz_ref):
    inverse = inverse_ref[...]
    half = jnp.dot(inverse, sum_ref[...] / total, precision=HI, preferred_element_type=F32)
    ritz_ref[...] = mm_t(half, inverse, HI)


def local(vectors, diag_tiles, pair_tiles, halo_tiles, halo_rows, pair_index, pair_count):
    k, own_rows = vectors.shape
    blocks, size, _ = diag_tiles.shape
    edges, peers = pair_index.shape[1], halo_rows.shape[1]
    total = float(own_rows * peers)
    rows = halo_rows[0]
    index = ((pair_index[0, :, 0], "s"), (pair_index[0, :, 1], "s"), (pair_count, "s"))
    block, spots, square = (blocks, k, size), (peers, k, size), (k, k)
    pair_tiles = pair_tiles.reshape(edges, 2, size, size)
    unit = 2 * k * size * size

    def room(shape, dtype):
        return pltpu.VMEM(shape, dtype)

    sems = pltpu.SemaphoreType.DMA((4,))
    [tiles] = call(tile_kernel, [((peers, size, size), BF16, "h")], [(halo_tiles, "h")], 1 << 20, 8 << 20)

    def exchange(out):
        return lax.all_to_all(out, "dom", 0, 0, tiled=True)

    def own(mode, cur, extra=(), ahead=()):
        ins = [*index, *ahead, (cur, "h"), (diag_tiles, "h"), (pair_tiles, "h"), *extra]
        [part] = call(functools.partial(local_kernel, mode), [(block, F32, "h")], ins, unit * (blocks + 2 * edges), 9 << 20)
        return part

    def halo(factor, arrived, part):
        return call(
            functools.partial(halo_kernel, factor),
            [(block, BF16, "a"), (spots, BF16, "a")],
            [(rows, "s"), (arrived, "v"), (tiles, "a"), (part, "a")],
            unit * peers,
            10 << 20,
            [room(tiles.shape, BF16), room(block, F32), room(block, F32), room(block, BF16), room(spots, BF16), sems],
        )

    def everywhere(x):
        near = [list(range(g, g + NODE)) for g in range(0, peers, NODE)]
        far = [list(range(g, peers, NODE)) for g in range(NODE)]
        for groups in (near, far):
            many = jnp.broadcast_to(x[None], (len(groups[0]), *x.shape))
            x = jnp.sum(lax.all_to_all(many, "dom", 0, 0, axis_index_groups=groups, tiled=True), axis=0)
        return x

    def other(x, step):
        return lax.ppermute(x, "dom", [(i, i ^ step) for i in range(peers)])

    def beside(x, work):
        x = x + other(x, 1)
        result = work(x)
        for step in (2, 8, 32):
            x = (x + other(x, step)) + (other(x, 2 * step) + other(x, 3 * step))
        return x, result

    def gram(cur):
        [value] = call(gram_kernel, [(square, F32, "h")], [(cur, "h")], 2 * k * k * own_rows, 1 << 20)
        return value

    def factor(value, cur, flat):
        outs = [(square, F32, "h"), (((k, own_rows) if flat else block), BF16, "h")]
        return call(functools.partial(factor_kernel, total, flat), outs, [(value, "h"), (cur, "h")], 1 << 24, 2 << 20)

    def image(cur, arrived, part, value, last):
        outs = [(square, F32, "h")] if last else [(block, F32, "a"), (block, BF16, "a"), (spots, BF16, "a")]
        ins = [(rows, "s"), (arrived, "v"), (tiles, "a"), (part, "a"), (cur, "a"), (value, "a")]
        scratch = [room(tiles.shape, BF16), room(block, F32), room(block, F32), room(block, BF16)]
        if not last:
            scratch += [room(block, BF16), room(spots, BF16)]
        return call(functools.partial(image_kernel, last), outs, ins, unit * peers, 10 << 20, [*scratch, sems])

    def filtered(prev, cur, out, centre, steps):
        for _ in range(steps):
            arrived = exchange(out)
            part = own("filter", cur, [(prev() if callable(prev) else prev, "h")], [(centre, "s")])
            prev, (cur, out) = cur, halo(2.0, arrived, part)
        return cur, out

    start, out = call(
        start_kernel,
        [(block, BF16, "h"), (spots, BF16, "a")],
        [(rows, "s"), (vectors, "h")],
        1 << 20,
        4 << 20,
        [room(spots, BF16), sems],
    )
    arrived = exchange(out)
    cur, out = halo(1.0, arrived, own("start", start))
    cur, out = filtered(start, cur, out, jnp.full((1, 1), FIRST_CENTRE, F32), 3)

    arrived = exchange(out)
    value, part = beside(gram(cur), lambda x: own("image", cur, [(x, "a")]))
    full, z, out = image(cur, arrived, part, value, False)

    arrived = exchange(out)
    inverse, begun = factor(value, cur, False)
    [value] = call(product_kernel, [(square, F32, "h")], [(cur, "h"), (full, "h")], 6 * k * k * own_rows, 2 << 20)
    value, part = beside(value, lambda x: own("image", z, [(x, "a")]))
    wide = [room(block, F32)] * 3 + [room(block, BF16)] * 4
    y, out, centre = call(
        functools.partial(turn_kernel, total),
        [(block, BF16, "a"), (spots, BF16, "a"), ((1, 1), F32, "s")],
        [(rows, "s"), (arrived, "v"), (tiles, "a"), (part, "a")]
        + [(full, "a"), (z, "a"), (cur, "a"), (begun, "a"), (inverse, "h"), (value, "h")],
        1 << 24,
        12 << 20,
        [room(tiles.shape, BF16), *wide, room(spots, BF16), sems, pltpu.SemaphoreType.DMA((5,))],
    )

    def first():
        ins = [(centre, "s"), (z, "h"), (cur, "h"), (inverse, "h")]
        return call(first_kernel, [(block, BF16, "h")], ins, 1 << 24, 2 << 20)[0]

    cur, out = filtered(first, y, out, centre, 2)

    arrived = exchange(out)
    value, part = beside(gram(cur), lambda x: own("image", cur, [(x, "a")]))
    [partial] = image(cur, arrived, part, value, True)
    inverse, basis = factor(value, cur, True)
    [ritz] = call(
        functools.partial(ritz_kernel, total), [(square, F32, "h")], [(inverse, "h"), (everywhere(partial), "h")], 1 << 20, 1 << 16
    )
    return basis, ritz


def solution(mesh):
    return jax.shard_map(
        local,
        mesh=mesh,
        in_specs=(
            P(None, "dom"),
            P("dom", None, None),
            P("dom", None, None, None),
            P("dom", None, None),
            P("dom", None),
            P("dom", None, None),
            P("dom"),
        ),
        out_specs=(P(None, "dom"), P()),
        check_vma=False,
    )
```

```python
import functools

import jax
import jax.numpy as jnp
from jax import lax
from jax.experimental import pallas as pl
from jax.experimental.pallas import tpu as pltpu
from jax.sharding import PartitionSpec as P

FIRST_CENTRE = -0.5
F32, BF16 = jnp.float32, jnp.bfloat16
HI = lax.Precision.HIGHEST
VM = pl.BlockSpec(memory_space=pltpu.VMEM)
SM = pl.BlockSpec(memory_space=pltpu.SMEM)


HBM = pl.BlockSpec(memory_space=pltpu.HBM)
NODE = 8
CHUNKS, WAVES = 8, 4


def call(body, outs, ins, flops, moved, scratch=()):
    place = {"a": pltpu.HBM, "v": pltpu.VMEM}
    spec = {"a": HBM, "v": VM, "h": VM, "s": SM}
    return pl.pallas_call(
        body,
        out_shape=[(place[kind] if kind in place else jax.ShapeDtypeStruct)(shape, dtype) for shape, dtype, kind in outs],
        in_specs=[spec[kind] for _, kind in ins],
        out_specs=[spec[kind] for _, _, kind in outs],
        scratch_shapes=list(scratch),
        cost_estimate=pl.CostEstimate(flops=flops, bytes_accessed=moved, transcendentals=0),
        compiler_params=pltpu.CompilerParams(vmem_limit_bytes=30 << 20),
    )(*[pltpu.with_memory_space_constraint(x, place[kind]) if kind in place else x for x, kind in ins])


def mm(a, b):
    return jnp.dot(a, b, preferred_element_type=F32)


def mm_t(a, b, precision=None):
    return lax.dot_general(a, b, (((1,), (1,)), ((), ())), precision=precision, preferred_element_type=F32)


def thirds(x):
    high = x.astype(BF16)
    rest = x - high.astype(F32)
    middle = rest.astype(BF16)
    return high, middle, (rest - middle.astype(F32)).astype(BF16)


def begin(source, target, sem):
    copy = pltpu.make_async_copy(source, target, sem)
    copy.start()
    return copy


def load(tiles_ref, tiles, sems):
    some = tiles.shape[0] // CHUNKS
    return [begin(tiles_ref.at[pl.ds(g * some, some)], tiles.at[pl.ds(g * some, some)], sems.at[g]) for g in range(CHUNKS)]


def send(rows_ref, blocks, tiles, coming, slots, out_ref, sems):
    some, ready = slots.shape[0] // WAVES, CHUNKS // WAVES
    copies = []
    for g in range(WAVES):
        for copy in coming[g * ready : (g + 1) * ready]:
            copy.wait()
        for p in range(g * some, (g + 1) * some):
            slots[p] = mm(blocks[rows_ref[0, p]], tiles[p]).astype(BF16)
        copies.append(begin(slots.at[pl.ds(g * some, some)], out_ref.at[pl.ds(g * some, some)], sems.at[g]))
    return copies


def receive(rows_ref, arrived_ref, acc):
    acc[...] = jnp.zeros(acc.shape, F32)
    for p in range(arrived_ref.shape[0]):
        acc[rows_ref[0, p]] += arrived_ref[p].astype(F32)


def start_kernel(rows_ref, vec_ref, tiles_ref, cur_ref, out_ref, tiles, vec, block, slots, loads, sems):
    first = begin(vec_ref, vec, sems.at[WAVES])
    coming = load(tiles_ref, tiles, loads)
    first.wait()
    width = block.shape[2]
    for r in range(block.shape[0]):
        block[r] = vec[:, r * width : (r + 1) * width]
    going = [begin(block, cur_ref, sems.at[WAVES])]
    going += send(rows_ref, block, tiles, coming, slots, out_ref, sems)
    for copy in going:
        copy.wait()


def local_kernel(mode, first_ref, second_ref, count_ref, *refs):
    if mode == "filter":
        centre_ref, cur_ref, diag_ref, pair_ref, prev_ref, acc_ref = refs
        centre = centre_ref[0, 0]
    else:
        cur_ref, diag_ref, pair_ref, acc_ref = refs
        centre = FIRST_CENTRE

    def own(r, _):
        block = cur_ref[r]
        value = mm(block, diag_ref[r])
        if mode != "image":
            value = value - centre * block.astype(F32)
        if mode == "filter":
            value = value - 0.5 * prev_ref[r].astype(F32)
        acc_ref[r] = value
        return _

    lax.fori_loop(0, cur_ref.shape[0], own, 0, unroll=4)
    count = count_ref[0]
    group = 4

    def step(i, _):
        parts = []
        for u in range(group):
            e = i * group + u
            live = jnp.where(e < count, 1.0, 0.0).astype(F32)
            r, c = first_ref[e], second_ref[e]
            parts.append((r, mm(cur_ref[c], pair_ref[e, 1]) * live))
            parts.append((c, mm(cur_ref[r], pair_ref[e, 0]) * live))
        for at, value in parts:
            acc_ref[at] += value
        return _

    lax.fori_loop(0, lax.div(count + (group - 1), group), step, 0)


def halo_kernel(factor, rows_ref, arrived_ref, tiles_ref, part_ref, cur_ref, out_ref, tiles, part, acc, block, slots, loads, sems):
    also = begin(part_ref, part, sems.at[WAVES])
    coming = load(tiles_ref, tiles, loads)
    receive(rows_ref, arrived_ref, acc)
    also.wait()
    block[...] = (factor * (acc[...] + part[...])).astype(BF16)
    going = [begin(block, cur_ref, sems.at[WAVES])]
    going += send(rows_ref, block, tiles, coming, slots, out_ref, sems)
    for copy in going:
        copy.wait()


def gram_kernel(cur_ref, gram_ref):
    value = jnp.zeros(gram_ref.shape, F32)
    for r in range(cur_ref.shape[0]):
        block = cur_ref[r]
        value = value + mm_t(block, block)
    gram_ref[...] = value


def corner(n):
    return lax.broadcasted_iota(jnp.int32, (n, n), 0), lax.broadcasted_iota(jnp.int32, (n, n), 1)


def packed(gram, product):
    n = gram.shape[0]
    row, col = corner(n)
    both = jnp.where(col >= row, gram, product)
    diagonal = jnp.sum(jnp.where(row == col, product, 0.0), axis=0, keepdims=True)
    last = jnp.concatenate([diagonal, jnp.zeros((1, n), F32)], axis=1)
    top = jnp.concatenate([both[: n // 2], both[n // 2 :]], axis=1)
    return jnp.concatenate([top, jnp.broadcast_to(last, (8, 2 * n))], axis=0)


def unpacked(sums):
    n = sums.shape[1] // 2
    row, col = corner(n)
    both = jnp.concatenate([sums[: n // 2, :n], sums[: n // 2, n:]], axis=0)
    turned = both.T
    diagonal = sums[n // 2 : n // 2 + 1, :n]
    gram = jnp.where(col >= row, both, turned)
    product = jnp.where(col < row, both, jnp.where(row == col, jnp.broadcast_to(diagonal, (n, n)), turned))
    return gram, product


def sums_kernel(keep, rows_ref, arrived_ref, part_ref, cur_ref, gram_ref, *refs):
    if keep:
        image_ref, sums_ref, part, acc, cur, sems = refs
    else:
        sums_ref, part, acc, cur, sems = refs
    also = begin(part_ref, part, sems.at[0])
    more = begin(cur_ref, cur, sems.at[1])
    receive(rows_ref, arrived_ref, acc)
    also.wait()
    acc[...] += part[...]
    if keep:
        going = begin(acc, image_ref, sems.at[2])
    more.wait()
    k = gram_ref.shape[0]
    value = jnp.zeros((k, k), F32)
    for r in range(acc.shape[0]):
        block = cur[r]
        for third in thirds(acc[r]):
            value = value + mm_t(block, third)
    sums_ref[...] = packed(gram_ref[...], value)
    if keep:
        going.wait()


def inverse_factor(gram):
    n = gram.shape[0]
    row = lax.broadcasted_iota(jnp.int32, (n, n), 0)
    col = lax.broadcasted_iota(jnp.int32, (n, n), 1)
    work = jnp.concatenate([gram, jnp.where(row == col, 1.0, 0.0).astype(F32)], axis=1)
    at = lax.broadcasted_iota(jnp.int32, work.shape, 0)
    for j in range(0, n, 2):
        first = jnp.broadcast_to(work[:, j : j + 1], work.shape)
        second = jnp.broadcast_to(work[:, j + 1 : j + 2], work.shape)
        over = 1.0 / first[j : j + 1]
        low = first[j + 1 : j + 2] * over
        upper = second[j : j + 1]
        under = 1.0 / (second[j + 1 : j + 2] - low * upper)
        below = work[j + 1 : j + 2] - low * work[j : j + 1]
        times = first * over
        again = jnp.where(at > j + 1, (second - times * upper) * under, 0.0)
        work = work - jnp.where(at > j, times, 0.0) * work[j : j + 1] - again * below
    pivots = jnp.sum(jnp.where(row == col, work[:, :n], 0.0), axis=1, keepdims=True)
    return work[:, n:] / jnp.sqrt(pivots)


def apply_square(parts, block):
    return mm(parts[0], block) + (mm(parts[1], block) + mm(parts[2], block))


def turn_kernel(total, rows_ref, sums_ref, cur_ref, image_ref, tiles_ref, next_ref, y_ref, out_ref, centre_ref, *scratch):
    cur, image, begun, block, tiles, slots, loads, sems = scratch
    first = begin(cur_ref, cur, sems.at[0])
    second = begin(image_ref, image, sems.at[1])
    coming = load(tiles_ref, tiles, loads)
    gram, product = unpacked(sums_ref[...])
    inverse = inverse_factor(gram / total)
    half = jnp.dot(inverse, product / total, precision=HI, preferred_element_type=F32)
    centre = jnp.sum(half * inverse) / inverse.shape[0] - 1.0
    centre_ref[0, 0] = centre
    parts = thirds(inverse)
    first.wait()
    second.wait()
    for r in range(cur.shape[0]):
        value = apply_square(parts, cur[r]).astype(BF16)
        begun[r] = value
        turned = jnp.dot(inverse, image[r], precision=HI, preferred_element_type=F32)
        block[r] = (turned - centre * value.astype(F32)).astype(BF16)
    going = [begin(begun, next_ref, sems.at[WAVES]), begin(block, y_ref, sems.at[WAVES + 1])]
    going += send(rows_ref, block, tiles, coming, slots, out_ref, sems)
    for copy in going:
        copy.wait()


def end_kernel(total, sums_ref, cur_ref, basis_ref, ritz_ref, cur, sems):
    coming = begin(cur_ref, cur, sems.at[0])
    width = cur.shape[2]
    gram, product = unpacked(sums_ref[...])
    inverse = inverse_factor(gram / total)
    parts = thirds(inverse)
    coming.wait()
    for r in range(cur.shape[0]):
        basis_ref[:, r * width : (r + 1) * width] = apply_square(parts, cur[r]).astype(BF16)
    half = jnp.dot(inverse, product / total, precision=HI, preferred_element_type=F32)
    ritz_ref[...] = mm_t(half, inverse, HI)


def local(vectors, diag_tiles, pair_tiles, halo_tiles, halo_rows, pair_index, pair_count):
    k, own_rows = vectors.shape
    blocks, size, _ = diag_tiles.shape
    edges, peers = pair_index.shape[1], halo_rows.shape[1]
    total = float(own_rows * peers)
    index = ((pair_index[0, :, 0], "s"), (pair_index[0, :, 1], "s"), (pair_count, "s"))
    block, spots, square = (blocks, k, size), (peers, k, size), (k, k)
    pair_tiles = pair_tiles.reshape(edges, 2, size, size)
    unit = 2 * k * size * size

    def room(shape, dtype):
        return pltpu.VMEM(shape, dtype)

    loads, sems = pltpu.SemaphoreType.DMA((CHUNKS,)), pltpu.SemaphoreType.DMA((WAVES + 2,))

    def exchange(out):
        return lax.all_to_all(out, "dom", 0, 0, tiled=True)

    def own(mode, cur, extra=(), ahead=()):
        ins = [*index, *ahead, (cur, "h"), (diag_tiles, "h"), (pair_tiles, "h"), *extra]
        [part] = call(functools.partial(local_kernel, mode), [(block, F32, "h")], ins, unit * (blocks + 2 * edges), 9 << 20)
        return part

    def halo(factor, arrived, part):
        return call(
            functools.partial(halo_kernel, factor),
            [(block, BF16, "a"), (spots, BF16, "a")],
            [(halo_rows, "s"), (arrived, "v"), (halo_tiles, "a"), (part, "a")],
            unit * peers,
            10 << 20,
            [room(halo_tiles.shape, BF16), room(block, F32), room(block, F32), room(block, BF16), room(spots, BF16), loads, sems],
        )

    def everywhere(x):
        near = [list(range(g, g + NODE)) for g in range(0, peers, NODE)]
        far = [list(range(g, peers, NODE)) for g in range(NODE)]
        for groups in (near, far):
            many = jnp.broadcast_to(x[None], (len(groups[0]), *x.shape))
            x = jnp.sum(lax.all_to_all(many, "dom", 0, 0, axis_index_groups=groups, tiled=True), axis=0)
        return x

    def sums(cur, arrived, part, keep):
        [gram] = call(gram_kernel, [(square, F32, "h")], [(cur, "h")], 2 * k * k * own_rows, 1 << 20)
        outs = [(block, F32, "a")] * keep + [((k // 2 + 8, 2 * k), F32, "h")]
        ins = [(halo_rows, "s"), (arrived, "v"), (part, "a"), (cur, "a"), (gram, "h")]
        scratch = [room(block, F32), room(block, F32), room(block, BF16), sems]
        *image, value = call(functools.partial(sums_kernel, keep), outs, ins, unit * peers, 10 << 20, scratch)
        return *image, everywhere(value)

    def filtered(prev, cur, out, centre):
        for _ in range(3):
            arrived = exchange(out)
            part = own("filter", cur, [(prev, "h")], [(centre, "s")])
            prev, (cur, out) = cur, halo(2.0, arrived, part)
        return cur, out

    start, out = call(
        start_kernel,
        [(block, BF16, "a"), (spots, BF16, "a")],
        [(halo_rows, "s"), (vectors, "a"), (halo_tiles, "a")],
        unit * peers,
        8 << 20,
        [room(halo_tiles.shape, BF16), room(vectors.shape, BF16), room(block, BF16), room(spots, BF16), loads, sems],
    )
    arrived = exchange(out)
    cur, out = halo(1.0, arrived, own("start", start))
    cur, out = filtered(start, cur, out, jnp.full((1, 1), FIRST_CENTRE, F32))

    arrived = exchange(out)
    image, value = sums(cur, arrived, own("image", cur), 1)
    begun, cur, out, centre = call(
        functools.partial(turn_kernel, total),
        [(block, BF16, "a"), (block, BF16, "a"), (spots, BF16, "a"), ((1, 1), F32, "s")],
        [(halo_rows, "s"), (value, "h"), (cur, "a"), (image, "a"), (halo_tiles, "a")],
        1 << 24,
        4 << 20,
        [room(block, BF16), room(block, F32), room(block, BF16), room(block, BF16)]
        + [room(halo_tiles.shape, BF16), room(spots, BF16), loads, sems],
    )
    cur, out = filtered(begun, cur, out, centre)

    arrived = exchange(out)
    [value] = sums(cur, arrived, own("image", cur), 0)
    return call(
        functools.partial(end_kernel, total),
        [((k, own_rows), BF16, "h"), (square, F32, "h")],
        [(value, "h"), (cur, "a")],
        1 << 24,
        2 << 20,
        [room(block, BF16), sems],
    )


def solution(mesh):
    return jax.shard_map(
        local,
        mesh=mesh,
        in_specs=(
            P(None, "dom"),
            P("dom", None, None),
            P("dom", None, None, None),
            P("dom", None, None),
            P("dom", None),
            P("dom", None, None),
            P("dom"),
        ),
        out_specs=(P(None, "dom"), P()),
        check_vma=False,
    )
```

```python
import functools

import jax
import jax.numpy as jnp
from jax import lax
from jax.experimental import pallas as pl
from jax.experimental.pallas import tpu as pltpu
from jax.sharding import PartitionSpec as P

FIRST_CENTRE = -0.5
F32, BF16 = jnp.float32, jnp.bfloat16
HI = lax.Precision.HIGHEST
VM = pl.BlockSpec(memory_space=pltpu.VMEM)
SM = pl.BlockSpec(memory_space=pltpu.SMEM)


HBM = pl.BlockSpec(memory_space=pltpu.HBM)
NODE = 8
CHUNKS, WAVES = 8, 4


def call(body, outs, ins, flops, moved, scratch=()):
    place = {"a": pltpu.HBM, "v": pltpu.VMEM}
    spec = {"a": HBM, "v": VM, "h": VM, "s": SM}
    return pl.pallas_call(
        body,
        out_shape=[(place[kind] if kind in place else jax.ShapeDtypeStruct)(shape, dtype) for shape, dtype, kind in outs],
        in_specs=[spec[kind] for _, kind in ins],
        out_specs=[spec[kind] for _, _, kind in outs],
        scratch_shapes=list(scratch),
        cost_estimate=pl.CostEstimate(flops=flops, bytes_accessed=moved, transcendentals=0),
        compiler_params=pltpu.CompilerParams(vmem_limit_bytes=30 << 20),
    )(*[pltpu.with_memory_space_constraint(x, place[kind]) if kind in place else x for x, kind in ins])


def mm(a, b):
    return jnp.dot(a, b, preferred_element_type=F32)


def mm_t(a, b, precision=None):
    return lax.dot_general(a, b, (((1,), (1,)), ((), ())), precision=precision, preferred_element_type=F32)


def thirds(x):
    high = x.astype(BF16)
    rest = x - high.astype(F32)
    middle = rest.astype(BF16)
    return high, middle, (rest - middle.astype(F32)).astype(BF16)


def begin(source, target, sem):
    copy = pltpu.make_async_copy(source, target, sem)
    copy.start()
    return copy


def load(tiles_ref, tiles, sems):
    some = tiles.shape[0] // CHUNKS
    return [begin(tiles_ref.at[pl.ds(g * some, some)], tiles.at[pl.ds(g * some, some)], sems.at[g]) for g in range(CHUNKS)]


def send(rows_ref, blocks, tiles, coming, slots, out_ref, sems):
    some, ready = slots.shape[0] // WAVES, CHUNKS // WAVES
    copies = []
    for g in range(WAVES):
        for copy in coming[g * ready : (g + 1) * ready]:
            copy.wait()
        for p in range(g * some, (g + 1) * some):
            slots[p] = mm(blocks[rows_ref[0, p]], tiles[p]).astype(BF16)
        copies.append(begin(slots.at[pl.ds(g * some, some)], out_ref.at[pl.ds(g * some, some)], sems.at[g]))
    return copies


def receive(rows_ref, arrived_ref, acc):
    acc[...] = jnp.zeros(acc.shape, F32)
    for p in range(arrived_ref.shape[0]):
        acc[rows_ref[0, p]] += arrived_ref[p].astype(F32)


def start_kernel(rows_ref, vec_ref, tiles_ref, cur_ref, out_ref, tiles, vec, block, slots, loads, sems):
    first = begin(vec_ref, vec, loads.at[CHUNKS])
    coming = load(tiles_ref, tiles, loads)
    first.wait()
    width = block.shape[2]
    for r in range(block.shape[0]):
        block[r] = vec[:, r * width : (r + 1) * width]
    going = [begin(block, cur_ref, loads.at[CHUNKS + 1])]
    going += send(rows_ref, block, tiles, coming, slots, out_ref, sems)
    for copy in going:
        copy.wait()


def local_kernel(mode, first_ref, second_ref, count_ref, *refs):
    if mode == "filter":
        centre_ref, cur_ref, diag_ref, pair_ref, prev_ref, acc_ref = refs
        centre = centre_ref[0, 0]
    else:
        cur_ref, diag_ref, pair_ref, acc_ref = refs
        centre = FIRST_CENTRE

    def own(r, _):
        block = cur_ref[r]
        value = mm(block, diag_ref[r])
        if mode != "image":
            value = value - centre * block.astype(F32)
        if mode == "filter":
            value = value - 0.5 * prev_ref[r].astype(F32)
        acc_ref[r] = value
        return _

    lax.fori_loop(0, cur_ref.shape[0], own, 0, unroll=4)
    count = count_ref[0]
    group = 4

    def step(i, _):
        parts = []
        for u in range(group):
            e = i * group + u
            live = jnp.where(e < count, 1.0, 0.0).astype(F32)
            r, c = first_ref[e], second_ref[e]
            parts.append((r, mm(cur_ref[c], pair_ref[e, 1]) * live))
            parts.append((c, mm(cur_ref[r], pair_ref[e, 0]) * live))
        for at, value in parts:
            acc_ref[at] += value
        return _

    lax.fori_loop(0, lax.div(count + (group - 1), group), step, 0)


def halo_kernel(factor, rows_ref, arrived_ref, tiles_ref, part_ref, cur_ref, out_ref, tiles, part, acc, block, slots, loads, sems):
    also = begin(part_ref, part, loads.at[CHUNKS])
    coming = load(tiles_ref, tiles, loads)
    receive(rows_ref, arrived_ref, acc)
    also.wait()
    block[...] = (factor * (acc[...] + part[...])).astype(BF16)
    going = [begin(block, cur_ref, loads.at[CHUNKS + 1])]
    going += send(rows_ref, block, tiles, coming, slots, out_ref, sems)
    for copy in going:
        copy.wait()


def gram_kernel(cur_ref, gram_ref):
    value = jnp.zeros(gram_ref.shape, F32)
    for r in range(cur_ref.shape[0]):
        block = cur_ref[r]
        value = value + mm_t(block, block)
    gram_ref[...] = value


def corner(n):
    return lax.broadcasted_iota(jnp.int32, (n, n), 0), lax.broadcasted_iota(jnp.int32, (n, n), 1)


def packed(gram, product):
    n = gram.shape[0]
    row, col = corner(n)
    both = jnp.where(col >= row, gram, product)
    diagonal = jnp.sum(jnp.where(row == col, product, 0.0), axis=0, keepdims=True)
    last = jnp.concatenate([diagonal, jnp.zeros((1, n), F32)], axis=1)
    top = jnp.concatenate([both[: n // 2], both[n // 2 :]], axis=1)
    return jnp.concatenate([top, jnp.broadcast_to(last, (8, 2 * n))], axis=0)


def unpacked(sums):
    n = sums.shape[1] // 2
    row, col = corner(n)
    both = jnp.concatenate([sums[: n // 2, :n], sums[: n // 2, n:]], axis=0)
    turned = both.T
    diagonal = sums[n // 2 : n // 2 + 1, :n]
    gram = jnp.where(col >= row, both, turned)
    product = jnp.where(col < row, both, jnp.where(row == col, jnp.broadcast_to(diagonal, (n, n)), turned))
    return gram, product


def sums_kernel(keep, rows_ref, arrived_ref, part_ref, cur_ref, gram_ref, *refs):
    if keep:
        image_ref, sums_ref, part, acc, cur, sems = refs
    else:
        sums_ref, part, acc, cur, sems = refs
    also = begin(part_ref, part, sems.at[0])
    more = begin(cur_ref, cur, sems.at[1])
    receive(rows_ref, arrived_ref, acc)
    also.wait()
    acc[...] += part[...]
    if keep:
        going = begin(acc, image_ref, sems.at[2])
    more.wait()
    k = gram_ref.shape[0]
    value = jnp.zeros((3 * k, k), F32)
    for r in range(acc.shape[0]):
        value = value + mm_t(jnp.concatenate(thirds(acc[r]), axis=0), cur[r])
    sums_ref[...] = packed(gram_ref[...], value[:k] + (value[k : 2 * k] + value[2 * k :]))
    if keep:
        going.wait()


def inverse_factor(gram):
    n = gram.shape[0]
    row = lax.broadcasted_iota(jnp.int32, (n, n), 0)
    col = lax.broadcasted_iota(jnp.int32, (n, n), 1)
    work = jnp.concatenate([gram, jnp.where(row == col, 1.0, 0.0).astype(F32)], axis=1)
    at = lax.broadcasted_iota(jnp.int32, work.shape, 0)
    for j in range(0, n, 2):
        first = jnp.broadcast_to(work[:, j : j + 1], work.shape)
        second = jnp.broadcast_to(work[:, j + 1 : j + 2], work.shape)
        over = 1.0 / first[j : j + 1]
        low = first[j + 1 : j + 2] * over
        upper = second[j : j + 1]
        under = 1.0 / (second[j + 1 : j + 2] - low * upper)
        below = work[j + 1 : j + 2] - low * work[j : j + 1]
        times = first * over
        again = jnp.where(at > j + 1, (second - times * upper) * under, 0.0)
        work = work - jnp.where(at > j, times, 0.0) * work[j : j + 1] - again * below
    pivots = jnp.sum(jnp.where(row == col, work[:, :n], 0.0), axis=1, keepdims=True)
    return work[:, n:] / jnp.sqrt(pivots)


def apply_square(stack, block):
    k = stack.shape[1]
    value = mm(stack, block)
    return value[:k] + (value[k : 2 * k] + value[2 * k :])


def apply_wide(stack, block):
    k = stack.shape[1]
    high, middle, low = thirds(block)
    first, second, third = mm(stack, high), mm(stack[: 2 * k], middle), mm(stack[:k], low)
    return first[:k] + ((first[k : 2 * k] + second[:k]) + (first[2 * k :] + second[k:] + third))


def turn_kernel(total, rows_ref, sums_ref, cur_ref, image_ref, tiles_ref, next_ref, y_ref, out_ref, centre_ref, *scratch):
    cur, image, begun, block, tiles, slots, loads, sems = scratch
    first = begin(cur_ref, cur, loads.at[CHUNKS])
    second = begin(image_ref, image, loads.at[CHUNKS + 1])
    coming = load(tiles_ref, tiles, loads)
    gram, product = unpacked(sums_ref[...])
    inverse = inverse_factor(gram / total)
    half = jnp.dot(inverse, product / total, precision=HI, preferred_element_type=F32)
    centre = jnp.sum(half * inverse) / inverse.shape[0] - 1.0
    centre_ref[0, 0] = centre
    stack = jnp.concatenate(thirds(inverse), axis=0)
    first.wait()
    second.wait()
    for r in range(cur.shape[0]):
        value = apply_square(stack, cur[r]).astype(BF16)
        begun[r] = value
        turned = apply_wide(stack, image[r])
        block[r] = (turned - centre * value.astype(F32)).astype(BF16)
    going = [begin(begun, next_ref, sems.at[WAVES]), begin(block, y_ref, sems.at[WAVES + 1])]
    going += send(rows_ref, block, tiles, coming, slots, out_ref, sems)
    for copy in going:
        copy.wait()


def end_kernel(total, sums_ref, cur_ref, basis_ref, ritz_ref, cur, sems):
    coming = begin(cur_ref, cur, sems.at[0])
    width = cur.shape[2]
    gram, product = unpacked(sums_ref[...])
    inverse = inverse_factor(gram / total)
    stack = jnp.concatenate(thirds(inverse), axis=0)
    coming.wait()
    for r in range(cur.shape[0]):
        basis_ref[:, r * width : (r + 1) * width] = apply_square(stack, cur[r]).astype(BF16)
    half = jnp.dot(inverse, product / total, precision=HI, preferred_element_type=F32)
    ritz_ref[...] = mm_t(half, inverse, HI)


def local(vectors, diag_tiles, pair_tiles, halo_tiles, halo_rows, pair_index, pair_count):
    k, own_rows = vectors.shape
    blocks, size, _ = diag_tiles.shape
    edges, peers = pair_index.shape[1], halo_rows.shape[1]
    total = float(own_rows * peers)
    index = ((pair_index[0, :, 0], "s"), (pair_index[0, :, 1], "s"), (pair_count, "s"))
    block, spots, square = (blocks, k, size), (peers, k, size), (k, k)
    pair_tiles = pair_tiles.reshape(edges, 2, size, size)
    unit = 2 * k * size * size

    def room(shape, dtype):
        return pltpu.VMEM(shape, dtype)

    loads, sems = pltpu.SemaphoreType.DMA((CHUNKS + 2,)), pltpu.SemaphoreType.DMA((WAVES + 2,))

    def exchange(out):
        return lax.all_to_all(out, "dom", 0, 0, tiled=True)

    def own(mode, cur, extra=(), ahead=()):
        ins = [*index, *ahead, (cur, "h"), (diag_tiles, "h"), (pair_tiles, "h"), *extra]
        [part] = call(functools.partial(local_kernel, mode), [(block, F32, "h")], ins, unit * (blocks + 2 * edges), 9 << 20)
        return part

    def halo(factor, arrived, part):
        return call(
            functools.partial(halo_kernel, factor),
            [(block, BF16, "a"), (spots, BF16, "a")],
            [(halo_rows, "s"), (arrived, "v"), (halo_tiles, "a"), (part, "a")],
            unit * peers,
            10 << 20,
            [room(halo_tiles.shape, BF16), room(block, F32), room(block, F32), room(block, BF16), room(spots, BF16), loads, sems],
        )

    def everywhere(x):
        near = [list(range(g, g + NODE)) for g in range(0, peers, NODE)]
        far = [list(range(g, peers, NODE)) for g in range(NODE)]
        for groups in (near, far):
            many = jnp.broadcast_to(x[None], (len(groups[0]), *x.shape))
            x = jnp.sum(lax.all_to_all(many, "dom", 0, 0, axis_index_groups=groups, tiled=True), axis=0)
        return x

    def sums(cur, arrived, part, keep):
        [gram] = call(gram_kernel, [(square, F32, "h")], [(cur, "h")], 2 * k * k * own_rows, 1 << 20)
        outs = [(block, F32, "a")] * keep + [((k // 2 + 8, 2 * k), F32, "h")]
        ins = [(halo_rows, "s"), (arrived, "v"), (part, "a"), (cur, "a"), (gram, "h")]
        scratch = [room(block, F32), room(block, F32), room(block, BF16), sems]
        *image, value = call(functools.partial(sums_kernel, keep), outs, ins, unit * peers, 10 << 20, scratch)
        return *image, everywhere(value)

    def filtered(prev, cur, out, centre):
        for _ in range(3):
            arrived = exchange(out)
            part = own("filter", cur, [(prev, "h")], [(centre, "s")])
            prev, (cur, out) = cur, halo(2.0, arrived, part)
        return cur, out

    start, out = call(
        start_kernel,
        [(block, BF16, "a"), (spots, BF16, "a")],
        [(halo_rows, "s"), (vectors, "a"), (halo_tiles, "a")],
        unit * peers,
        8 << 20,
        [room(halo_tiles.shape, BF16), room(vectors.shape, BF16), room(block, BF16), room(spots, BF16), loads, sems],
    )
    arrived = exchange(out)
    cur, out = halo(1.0, arrived, own("start", start))
    cur, out = filtered(start, cur, out, jnp.full((1, 1), FIRST_CENTRE, F32))

    arrived = exchange(out)
    image, value = sums(cur, arrived, own("image", cur), 1)
    begun, cur, out, centre = call(
        functools.partial(turn_kernel, total),
        [(block, BF16, "a"), (block, BF16, "a"), (spots, BF16, "a"), ((1, 1), F32, "s")],
        [(halo_rows, "s"), (value, "h"), (cur, "a"), (image, "a"), (halo_tiles, "a")],
        1 << 24,
        4 << 20,
        [room(block, BF16), room(block, F32), room(block, BF16), room(block, BF16)]
        + [room(halo_tiles.shape, BF16), room(spots, BF16), loads, sems],
    )
    cur, out = filtered(begun, cur, out, centre)

    arrived = exchange(out)
    [value] = sums(cur, arrived, own("image", cur), 0)
    return call(
        functools.partial(end_kernel, total),
        [((k, own_rows), BF16, "h"), (square, F32, "h")],
        [(value, "h"), (cur, "a")],
        1 << 24,
        2 << 20,
        [room(block, BF16), sems],
    )


def solution(mesh):
    return jax.shard_map(
        local,
        mesh=mesh,
        in_specs=(
            P(None, "dom"),
            P("dom", None, None),
            P("dom", None, None, None),
            P("dom", None, None),
            P("dom", None),
            P("dom", None, None),
            P("dom"),
        ),
        out_specs=(P(None, "dom"), P()),
        check_vma=False,
    )
```

```python
import functools

import jax
import jax.numpy as jnp
from jax import lax
from jax.experimental import pallas as pl
from jax.experimental.pallas import tpu as pltpu
from jax.sharding import PartitionSpec as P

FIRST_CENTRE = -0.5
F32, BF16 = jnp.float32, jnp.bfloat16
HI = lax.Precision.HIGHEST
VM = pl.BlockSpec(memory_space=pltpu.VMEM)
SM = pl.BlockSpec(memory_space=pltpu.SMEM)


HBM = pl.BlockSpec(memory_space=pltpu.HBM)
NODE = 8
CHUNKS, WAVES = 8, 4


def call(body, outs, ins, flops, moved, scratch=()):
    place = {"a": pltpu.HBM, "v": pltpu.VMEM}
    spec = {"a": HBM, "v": VM, "h": VM, "s": SM}
    return pl.pallas_call(
        body,
        out_shape=[(place[kind] if kind in place else jax.ShapeDtypeStruct)(shape, dtype) for shape, dtype, kind in outs],
        in_specs=[spec[kind] for _, kind in ins],
        out_specs=[spec[kind] for _, _, kind in outs],
        scratch_shapes=list(scratch),
        cost_estimate=pl.CostEstimate(flops=flops, bytes_accessed=moved, transcendentals=0),
        compiler_params=pltpu.CompilerParams(vmem_limit_bytes=30 << 20),
    )(*[pltpu.with_memory_space_constraint(x, place[kind]) if kind in place else x for x, kind in ins])


def mm(a, b):
    return jnp.dot(a, b, preferred_element_type=F32)


def mm_t(a, b, precision=None):
    return lax.dot_general(a, b, (((1,), (1,)), ((), ())), precision=precision, preferred_element_type=F32)


def thirds(x):
    high = x.astype(BF16)
    rest = x - high.astype(F32)
    middle = rest.astype(BF16)
    return high, middle, (rest - middle.astype(F32)).astype(BF16)


def begin(source, target, sem):
    copy = pltpu.make_async_copy(source, target, sem)
    copy.start()
    return copy


def load(tiles_ref, tiles, sems):
    some = tiles.shape[0] // CHUNKS
    return [begin(tiles_ref.at[pl.ds(g * some, some)], tiles.at[pl.ds(g * some, some)], sems.at[g]) for g in range(CHUNKS)]


def send(rows_ref, blocks, tiles, coming, slots, out_ref, sems):
    some, ready = slots.shape[0] // WAVES, CHUNKS // WAVES
    copies = []
    for g in range(WAVES):
        for copy in coming[g * ready : (g + 1) * ready]:
            copy.wait()
        for p in range(g * some, (g + 1) * some):
            slots[p] = mm(blocks[rows_ref[0, p]], tiles[p]).astype(BF16)
        copies.append(begin(slots.at[pl.ds(g * some, some)], out_ref.at[pl.ds(g * some, some)], sems.at[g]))
    return copies


def receive(rows_ref, arrived_ref, acc):
    acc[...] = jnp.zeros(acc.shape, F32)
    for p in range(arrived_ref.shape[0]):
        acc[rows_ref[0, p]] += arrived_ref[p].astype(F32)


def start_kernel(rows_ref, vec_ref, tiles_ref, cur_ref, out_ref, tiles, vec, block, slots, loads, sems):
    first = begin(vec_ref, vec, loads.at[CHUNKS])
    coming = load(tiles_ref, tiles, loads)
    first.wait()
    width = block.shape[2]
    for r in range(block.shape[0]):
        block[r] = vec[:, r * width : (r + 1) * width]
    going = [begin(block, cur_ref, loads.at[CHUNKS + 1])]
    going += send(rows_ref, block, tiles, coming, slots, out_ref, sems)
    for copy in going:
        copy.wait()


def local_kernel(mode, first_ref, second_ref, count_ref, *refs):
    if mode == "filter":
        centre_ref, cur_ref, diag_ref, pair_ref, prev_ref, acc_ref = refs
        centre = centre_ref[0, 0]
    else:
        cur_ref, diag_ref, pair_ref, acc_ref = refs
        centre = FIRST_CENTRE

    def own(r, _):
        block = cur_ref[r]
        value = mm(block, diag_ref[r])
        if mode != "image":
            value = value - centre * block.astype(F32)
        if mode == "filter":
            value = value - 0.5 * prev_ref[r].astype(F32)
        acc_ref[r] = value
        return _

    lax.fori_loop(0, cur_ref.shape[0], own, 0, unroll=4)
    count = count_ref[0]
    group = 4

    def step(i, _):
        parts = []
        for u in range(group):
            e = i * group + u
            live = jnp.where(e < count, 1.0, 0.0).astype(F32)
            r, c = first_ref[e], second_ref[e]
            parts.append((r, mm(cur_ref[c], pair_ref[e, 1]) * live))
            parts.append((c, mm(cur_ref[r], pair_ref[e, 0]) * live))
        for at, value in parts:
            acc_ref[at] += value
        return _

    lax.fori_loop(0, lax.div(count + (group - 1), group), step, 0)


def halo_kernel(factor, rows_ref, arrived_ref, tiles_ref, part_ref, cur_ref, out_ref, tiles, part, acc, block, slots, loads, sems):
    also = begin(part_ref, part, loads.at[CHUNKS])
    coming = load(tiles_ref, tiles, loads)
    receive(rows_ref, arrived_ref, acc)
    also.wait()
    block[...] = (factor * (acc[...] + part[...])).astype(BF16)
    going = [begin(block, cur_ref, loads.at[CHUNKS + 1])]
    going += send(rows_ref, block, tiles, coming, slots, out_ref, sems)
    for copy in going:
        copy.wait()


def gram_kernel(cur_ref, gram_ref):
    value = jnp.zeros(gram_ref.shape, F32)
    for r in range(cur_ref.shape[0]):
        block = cur_ref[r]
        value = value + mm_t(block, block)
    gram_ref[...] = value


def corner(n):
    return lax.broadcasted_iota(jnp.int32, (n, n), 0), lax.broadcasted_iota(jnp.int32, (n, n), 1)


def packed(gram, product):
    n = gram.shape[0]
    row, col = corner(n)
    both = jnp.where(col >= row, gram, product)
    diagonal = jnp.sum(jnp.where(row == col, product, 0.0), axis=0, keepdims=True)
    last = jnp.concatenate([diagonal, jnp.zeros((1, n), F32)], axis=1)
    top = jnp.concatenate([both[: n // 2], both[n // 2 :]], axis=1)
    return jnp.concatenate([top, jnp.broadcast_to(last, (8, 2 * n))], axis=0)


def unpacked(sums):
    n = sums.shape[1] // 2
    row, col = corner(n)
    both = jnp.concatenate([sums[: n // 2, :n], sums[: n // 2, n:]], axis=0)
    turned = both.T
    diagonal = sums[n // 2 : n // 2 + 1, :n]
    gram = jnp.where(col >= row, both, turned)
    product = jnp.where(col < row, both, jnp.where(row == col, jnp.broadcast_to(diagonal, (n, n)), turned))
    return gram, product


def sums_kernel(keep, rows_ref, arrived_ref, part_ref, cur_ref, gram_ref, *refs):
    if keep:
        image_ref, sums_ref, part, acc, cur, sems = refs
    else:
        sums_ref, part, acc, cur, sems = refs
    also = begin(part_ref, part, sems.at[0])
    more = begin(cur_ref, cur, sems.at[1])
    receive(rows_ref, arrived_ref, acc)
    also.wait()
    acc[...] += part[...]
    if keep:
        going = begin(acc, image_ref, sems.at[2])
    more.wait()
    k = gram_ref.shape[0]
    value = jnp.zeros((3 * k, k), F32)
    for r in range(acc.shape[0]):
        value = value + mm_t(jnp.concatenate(thirds(acc[r]), axis=0), cur[r])
    sums_ref[...] = packed(gram_ref[...], value[:k] + (value[k : 2 * k] + value[2 * k :]))
    if keep:
        going.wait()


def inverse_factor(gram):
    n, some = gram.shape[0], 8
    row, col = corner(n)
    work = jnp.concatenate([gram, jnp.where(row == col, 1.0, 0.0).astype(F32)], axis=1)
    parts = [work[b : b + some] for b in range(0, n, some)]
    at = lax.broadcasted_iota(jnp.int32, parts[0].shape, 0)
    for j in range(0, n, 2):
        own, o = j // some, j % some
        first = [jnp.broadcast_to(part[:, j : j + 1], part.shape) for part in parts[own:]]
        second = [jnp.broadcast_to(part[:, j + 1 : j + 2], part.shape) for part in parts[own:]]
        over = 1.0 / first[0][o : o + 1]
        low = first[0][o + 1 : o + 2] * over
        upper = second[0][o : o + 1]
        under = 1.0 / (second[0][o + 1 : o + 2] - low * upper)
        above = parts[own][o : o + 1]
        below = parts[own][o + 1 : o + 2] - low * above
        for i, part in enumerate(parts[own:]):
            times = first[i] * over
            again = (second[i] - times * upper) * under
            if i == 0:
                times, again = jnp.where(at > o, times, 0.0), jnp.where(at > o + 1, again, 0.0)
            parts[own + i] = part - times * above - again * below
    work = jnp.concatenate(parts, axis=0)
    pivots = jnp.sum(jnp.where(row == col, work[:, :n], 0.0), axis=1, keepdims=True)
    return work[:, n:] / jnp.sqrt(pivots)


def apply_square(stack, block):
    k = stack.shape[1]
    value = mm(stack, block)
    return value[:k] + (value[k : 2 * k] + value[2 * k :])


def apply_wide(stack, block):
    k = stack.shape[1]
    high, middle, low = thirds(block)
    first, second, third = mm(stack, high), mm(stack[: 2 * k], middle), mm(stack[:k], low)
    return first[:k] + ((first[k : 2 * k] + second[:k]) + (first[2 * k :] + second[k:] + third))


def shift_kernel(rows_ref, image_ref, cur_ref, tiles_ref, near_ref, z_ref, out_ref, image, cur, block, tiles, slots, loads, sems):
    del near_ref
    first = begin(cur_ref, cur, loads.at[CHUNKS])
    second = begin(image_ref, image, loads.at[CHUNKS + 1])
    coming = load(tiles_ref, tiles, loads)
    first.wait()
    second.wait()
    block[...] = (image[...] - FIRST_CENTRE * cur[...].astype(F32)).astype(BF16)
    going = [begin(block, z_ref, loads.at[CHUNKS])]
    going += send(rows_ref, block, tiles, coming, slots, out_ref, sems)
    for copy in going:
        copy.wait()


def factor_kernel(total, sums_ref, cur_ref, image_ref, z_ref, part_ref, inverse_ref, y_ref, centre_ref, rest_ref):
    gram, product = unpacked(sums_ref[...])
    inverse = inverse_factor(gram / total)
    inverse_ref[...] = inverse
    half = jnp.dot(inverse, product / total, precision=HI, preferred_element_type=F32)
    centre = jnp.sum(half * inverse) / inverse.shape[0] - 1.0
    centre_ref[0, 0] = centre
    change = centre - FIRST_CENTRE
    stack = jnp.concatenate(thirds(inverse), axis=0)
    for r in range(cur_ref.shape[0]):
        block = cur_ref[r]
        begun = apply_square(stack, block).astype(BF16)
        moved = z_ref[r].astype(F32) - change * block.astype(F32)
        y_ref[r] = apply_wide(stack, moved).astype(BF16)
        rest = apply_wide(stack, part_ref[r] - change * image_ref[r] - centre * moved)
        rest_ref[r] = 2.0 * rest - begun.astype(F32)


def turn_kernel(rows_ref, arrived_ref, tiles_ref, part_ref, inverse_ref, cur_ref, out_ref, tiles, part, acc, block, slots, loads, sems):
    also = begin(part_ref, part, loads.at[CHUNKS])
    coming = load(tiles_ref, tiles, loads)
    receive(rows_ref, arrived_ref, acc)
    stack = jnp.concatenate(thirds(inverse_ref[...]), axis=0)
    also.wait()
    for r in range(block.shape[0]):
        block[r] = (2.0 * apply_wide(stack, acc[r]) + part[r]).astype(BF16)
    going = [begin(block, cur_ref, loads.at[CHUNKS + 1])]
    going += send(rows_ref, block, tiles, coming, slots, out_ref, sems)
    for copy in going:
        copy.wait()


def end_kernel(total, sums_ref, cur_ref, basis_ref, ritz_ref, cur, sems):
    coming = begin(cur_ref, cur, sems.at[0])
    width = cur.shape[2]
    gram, product = unpacked(sums_ref[...])
    inverse = inverse_factor(gram / total)
    stack = jnp.concatenate(thirds(inverse), axis=0)
    coming.wait()
    for r in range(cur.shape[0]):
        basis_ref[:, r * width : (r + 1) * width] = apply_square(stack, cur[r]).astype(BF16)
    half = jnp.dot(inverse, product / total, precision=HI, preferred_element_type=F32)
    ritz_ref[...] = mm_t(half, inverse, HI)


def local(vectors, diag_tiles, pair_tiles, halo_tiles, halo_rows, pair_index, pair_count):
    k, own_rows = vectors.shape
    blocks, size, _ = diag_tiles.shape
    edges, peers = pair_index.shape[1], halo_rows.shape[1]
    total = float(own_rows * peers)
    index = ((pair_index[0, :, 0], "s"), (pair_index[0, :, 1], "s"), (pair_count, "s"))
    block, spots, square = (blocks, k, size), (peers, k, size), (k, k)
    pair_tiles = pair_tiles.reshape(edges, 2, size, size)
    unit = 2 * k * size * size

    def room(shape, dtype):
        return pltpu.VMEM(shape, dtype)

    loads, sems = pltpu.SemaphoreType.DMA((CHUNKS + 2,)), pltpu.SemaphoreType.DMA((WAVES + 2,))

    def exchange(out):
        return lax.all_to_all(out, "dom", 0, 0, tiled=True)

    def own(mode, cur, extra=(), ahead=()):
        ins = [*index, *ahead, (cur, "h"), (diag_tiles, "h"), (pair_tiles, "h"), *extra]
        [part] = call(functools.partial(local_kernel, mode), [(block, F32, "h")], ins, unit * (blocks + 2 * edges), 9 << 20)
        return part

    def halo(factor, arrived, part):
        return call(
            functools.partial(halo_kernel, factor),
            [(block, BF16, "a"), (spots, BF16, "a")],
            [(halo_rows, "s"), (arrived, "v"), (halo_tiles, "a"), (part, "a")],
            unit * peers,
            10 << 20,
            [room(halo_tiles.shape, BF16), room(block, F32), room(block, F32), room(block, BF16), room(spots, BF16), loads, sems],
        )

    def everywhere(x, between=None):
        near = [list(range(g, g + NODE)) for g in range(0, peers, NODE)]
        far = [list(range(g, peers, NODE)) for g in range(NODE)]
        result = None
        for groups in (near, far):
            if between and groups is far:
                result = between(x)
            many = jnp.broadcast_to(x[None], (len(groups[0]), *x.shape))
            x = jnp.sum(lax.all_to_all(many, "dom", 0, 0, axis_index_groups=groups, tiled=True), axis=0)
        return x, result

    def sums(cur, arrived, part, keep):
        [gram] = call(gram_kernel, [(square, F32, "h")], [(cur, "h")], 2 * k * k * own_rows, 1 << 20)
        outs = [(block, F32, "a")] * keep + [((k // 2 + 8, 2 * k), F32, "h")]
        ins = [(halo_rows, "s"), (arrived, "v"), (part, "a"), (cur, "a"), (gram, "h")]
        scratch = [room(block, F32), room(block, F32), room(block, BF16), sems]
        *image, value = call(functools.partial(sums_kernel, keep), outs, ins, unit * peers, 10 << 20, scratch)
        return *image, value

    def filtered(prev, cur, out, centre, steps):
        for _ in range(steps):
            arrived = exchange(out)
            part = own("filter", cur, [(prev, "h")], [(centre, "s")])
            prev, (cur, out) = cur, halo(2.0, arrived, part)
        return cur, out

    start, out = call(
        start_kernel,
        [(block, BF16, "a"), (spots, BF16, "a")],
        [(halo_rows, "s"), (vectors, "a"), (halo_tiles, "a")],
        unit * peers,
        8 << 20,
        [room(halo_tiles.shape, BF16), room(vectors.shape, BF16), room(block, BF16), room(spots, BF16), loads, sems],
    )
    arrived = exchange(out)
    cur, out = halo(1.0, arrived, own("start", start))
    cur, out = filtered(start, cur, out, jnp.full((1, 1), FIRST_CENTRE, F32), 3)

    arrived = exchange(out)
    image, value = sums(cur, arrived, own("image", cur), 1)

    def shift(near):
        return call(
            shift_kernel,
            [(block, BF16, "a"), (spots, BF16, "a")],
            [(halo_rows, "s"), (image, "a"), (cur, "a"), (halo_tiles, "a"), (near, "a")],
            unit * peers,
            8 << 20,
            [room(block, F32), room(block, BF16), room(block, BF16), room(halo_tiles.shape, BF16), room(spots, BF16), loads, sems],
        )

    value, (z, out) = everywhere(value, shift)
    arrived = exchange(out)
    inverse, first, centre, rest = call(
        functools.partial(factor_kernel, total),
        [(square, F32, "h"), (block, BF16, "h"), ((1, 1), F32, "s"), (block, F32, "h")],
        [(value, "h"), (cur, "h"), (image, "h"), (z, "h"), (own("image", z), "h")],
        1 << 24,
        4 << 20,
    )
    cur, out = call(
        turn_kernel,
        [(block, BF16, "a"), (spots, BF16, "a")],
        [(halo_rows, "s"), (arrived, "v"), (halo_tiles, "a"), (rest, "a"), (inverse, "h")],
        unit * peers,
        10 << 20,
        [room(halo_tiles.shape, BF16), room(block, F32), room(block, F32), room(block, BF16), room(spots, BF16), loads, sems],
    )
    cur, out = filtered(first, cur, out, centre, 2)

    arrived = exchange(out)
    [value] = sums(cur, arrived, own("image", cur), 0)
    value, _ = everywhere(value)
    return call(
        functools.partial(end_kernel, total),
        [((k, own_rows), BF16, "h"), (square, F32, "h")],
        [(value, "h"), (cur, "a")],
        1 << 24,
        2 << 20,
        [room(block, BF16), sems],
    )


def solution(mesh):
    return jax.shard_map(
        local,
        mesh=mesh,
        in_specs=(
            P(None, "dom"),
            P("dom", None, None),
            P("dom", None, None, None),
            P("dom", None, None),
            P("dom", None),
            P("dom", None, None),
            P("dom"),
        ),
        out_specs=(P(None, "dom"), P()),
        check_vma=False,
    )
```

```python
import functools

import jax
import jax.numpy as jnp
from jax import lax
from jax.experimental import pallas as pl
from jax.experimental.pallas import tpu as pltpu
from jax.sharding import PartitionSpec as P

FIRST_CENTRE = -0.5
F32, BF16 = jnp.float32, jnp.bfloat16
HI = lax.Precision.HIGHEST
VM = pl.BlockSpec(memory_space=pltpu.VMEM)
SM = pl.BlockSpec(memory_space=pltpu.SMEM)


HBM = pl.BlockSpec(memory_space=pltpu.HBM)
NODE = 8
CHUNKS, WAVES = 8, 4


def call(body, outs, ins, flops, moved, scratch=()):
    place = {"a": pltpu.HBM, "v": pltpu.VMEM}
    spec = {"a": HBM, "v": VM, "h": VM, "s": SM}
    return pl.pallas_call(
        body,
        out_shape=[(place[kind] if kind in place else jax.ShapeDtypeStruct)(shape, dtype) for shape, dtype, kind in outs],
        in_specs=[spec[kind] for _, kind in ins],
        out_specs=[spec[kind] for _, _, kind in outs],
        scratch_shapes=list(scratch),
        cost_estimate=pl.CostEstimate(flops=flops, bytes_accessed=moved, transcendentals=0),
        compiler_params=pltpu.CompilerParams(vmem_limit_bytes=30 << 20),
    )(*[pltpu.with_memory_space_constraint(x, place[kind]) if kind in place else x for x, kind in ins])


def mm(a, b):
    return jnp.dot(a, b, preferred_element_type=F32)


def mm_t(a, b, precision=None):
    return lax.dot_general(a, b, (((1,), (1,)), ((), ())), precision=precision, preferred_element_type=F32)


def thirds(x):
    high = x.astype(BF16)
    rest = x - high.astype(F32)
    middle = rest.astype(BF16)
    return high, middle, (rest - middle.astype(F32)).astype(BF16)


def begin(source, target, sem):
    copy = pltpu.make_async_copy(source, target, sem)
    copy.start()
    return copy


def load(tiles_ref, tiles, sems):
    some = tiles.shape[0] // CHUNKS
    return [begin(tiles_ref.at[pl.ds(g * some, some)], tiles.at[pl.ds(g * some, some)], sems.at[g]) for g in range(CHUNKS)]


def send(rows_ref, blocks, tiles, coming, slots, out_ref, sems):
    some, ready = slots.shape[0] // WAVES, CHUNKS // WAVES
    copies = []
    for g in range(WAVES):
        for copy in coming[g * ready : (g + 1) * ready]:
            copy.wait()
        for p in range(g * some, (g + 1) * some):
            slots[p] = mm(blocks[rows_ref[0, p]], tiles[p]).astype(BF16)
        copies.append(begin(slots.at[pl.ds(g * some, some)], out_ref.at[pl.ds(g * some, some)], sems.at[g]))
    return copies


def receive(rows_ref, arrived_ref, acc):
    acc[...] = jnp.zeros(acc.shape, F32)
    for p in range(arrived_ref.shape[0]):
        acc[rows_ref[0, p]] += arrived_ref[p].astype(F32)


def start_kernel(rows_ref, vec_ref, tiles_ref, cur_ref, out_ref, rows, tiles, vec, block, slots, loads, sems):
    first = begin(vec_ref, vec, loads.at[CHUNKS])
    also = begin(rows_ref, rows, loads.at[CHUNKS + 1])
    coming = load(tiles_ref, tiles, loads)
    first.wait()
    width = block.shape[2]
    for r in range(block.shape[0]):
        block[r] = vec[:, r * width : (r + 1) * width]
    also.wait()
    going = [begin(block, cur_ref, loads.at[CHUNKS + 1])]
    going += send(rows, block, tiles, coming, slots, out_ref, sems)
    for copy in going:
        copy.wait()


def local_kernel(mode, first_ref, second_ref, count_ref, *refs):
    if mode == "filter":
        centre_ref, cur_ref, diag_ref, pair_ref, prev_ref, acc_ref = refs
        centre = centre_ref[0, 0]
    else:
        cur_ref, diag_ref, pair_ref, acc_ref = refs
        centre = FIRST_CENTRE

    def own(r, _):
        block = cur_ref[r]
        value = mm(block, diag_ref[r])
        if mode != "image":
            value = value - centre * block.astype(F32)
        if mode == "filter":
            value = value - 0.5 * prev_ref[r].astype(F32)
        acc_ref[r] = value
        return _

    lax.fori_loop(0, cur_ref.shape[0], own, 0, unroll=4)
    count = count_ref[0]
    group = 4

    def step(i, _):
        parts = []
        for u in range(group):
            e = i * group + u
            live = jnp.where(e < count, 1.0, 0.0).astype(F32)
            r, c = first_ref[e], second_ref[e]
            parts.append((r, mm(cur_ref[c], pair_ref[e, 1]) * live))
            parts.append((c, mm(cur_ref[r], pair_ref[e, 0]) * live))
        for at, value in parts:
            acc_ref[at] += value
        return _

    lax.fori_loop(0, lax.div(count + (group - 1), group), step, 0)


def halo_kernel(factor, rows_ref, arrived_ref, tiles_ref, part_ref, cur_ref, out_ref, tiles, part, acc, block, slots, loads, sems):
    also = begin(part_ref, part, loads.at[CHUNKS])
    coming = load(tiles_ref, tiles, loads)
    receive(rows_ref, arrived_ref, acc)
    also.wait()
    block[...] = (factor * (acc[...] + part[...])).astype(BF16)
    going = [begin(block, cur_ref, loads.at[CHUNKS + 1])]
    going += send(rows_ref, block, tiles, coming, slots, out_ref, sems)
    for copy in going:
        copy.wait()


def gram_kernel(cur_ref, gram_ref):
    value = jnp.zeros(gram_ref.shape, F32)
    for r in range(cur_ref.shape[0]):
        block = cur_ref[r]
        value = value + mm_t(block, block)
    gram_ref[...] = value


def corner(n):
    return lax.broadcasted_iota(jnp.int32, (n, n), 0), lax.broadcasted_iota(jnp.int32, (n, n), 1)


def packed(gram, product):
    n = gram.shape[0]
    row, col = corner(n)
    both = jnp.where(col >= row, gram, product)
    diagonal = jnp.sum(jnp.where(row == col, product, 0.0), axis=0, keepdims=True)
    last = jnp.concatenate([diagonal, jnp.zeros((1, n), F32)], axis=1)
    top = jnp.concatenate([both[: n // 2], both[n // 2 :]], axis=1)
    return jnp.concatenate([top, jnp.broadcast_to(last, (8, 2 * n))], axis=0)


def unpacked(sums):
    n = sums.shape[1] // 2
    row, col = corner(n)
    both = jnp.concatenate([sums[: n // 2, :n], sums[: n // 2, n:]], axis=0)
    turned = both.T
    diagonal = sums[n // 2 : n // 2 + 1, :n]
    gram = jnp.where(col >= row, both, turned)
    product = jnp.where(col < row, both, jnp.where(row == col, jnp.broadcast_to(diagonal, (n, n)), turned))
    return gram, product


def sums_kernel(keep, rows_ref, arrived_ref, part_ref, cur_ref, gram_ref, *refs):
    if keep:
        image_ref, sums_ref, part, acc, cur, sems = refs
    else:
        sums_ref, part, acc, cur, sems = refs
    also = begin(part_ref, part, sems.at[0])
    more = begin(cur_ref, cur, sems.at[1])
    receive(rows_ref, arrived_ref, acc)
    also.wait()
    acc[...] += part[...]
    if keep:
        going = begin(acc, image_ref, sems.at[2])
    more.wait()
    k = gram_ref.shape[0]
    value = jnp.zeros((3 * k, k), F32)
    for r in range(acc.shape[0]):
        value = value + mm_t(jnp.concatenate(thirds(acc[r]), axis=0), cur[r])
    sums_ref[...] = packed(gram_ref[...], value[:k] + (value[k : 2 * k] + value[2 * k :]))
    if keep:
        going.wait()


def inverse_factor(gram):
    n, some = gram.shape[0], 8
    row, col = corner(n)
    work = jnp.concatenate([gram, jnp.where(row == col, 1.0, 0.0).astype(F32)], axis=1)
    parts = [work[b : b + some] for b in range(0, n, some)]
    at = lax.broadcasted_iota(jnp.int32, parts[0].shape, 0)
    for own in range(len(parts)):
        live = parts[own:]
        columns = [[jnp.broadcast_to(part[:, own * some + g : own * some + g + 1], part.shape) for part in live] for g in range(some)]
        pivot = [[columns[h][0][g : g + 1] for h in range(some)] for g in range(some)]
        rows = [live[0][g : g + 1] for g in range(some)]
        over = []
        for g in range(some):
            over.append(1.0 / pivot[g][g])
            for h in range(g + 1, some):
                low = pivot[h][g] * over[g]
                rows[h] = rows[h] - low * rows[g]
                for x in range(g + 1, some):
                    pivot[h][x] = pivot[h][x] - low * pivot[g][x]
        for i, part in enumerate(live):
            times = []
            for g in range(some):
                value = columns[g][i]
                for h in range(g):
                    value = value - times[h] * pivot[h][g]
                times.append(value * over[g])
            for g in range(some):
                part = part - (jnp.where(at > g, times[g], 0.0) if i == 0 else times[g]) * rows[g]
            parts[own + i] = part
    work = jnp.concatenate(parts, axis=0)
    pivots = jnp.sum(jnp.where(row == col, work[:, :n], 0.0), axis=1, keepdims=True)
    return work[:, n:] / jnp.sqrt(pivots)


def apply_square(stack, block):
    k = stack.shape[1]
    value = mm(stack, block)
    return value[:k] + (value[k : 2 * k] + value[2 * k :])


def apply_wide(stack, block):
    k = stack.shape[1]
    high, middle, low = thirds(block)
    first, second, third = mm(stack, high), mm(stack[: 2 * k], middle), mm(stack[:k], low)
    return first[:k] + ((first[k : 2 * k] + second[:k]) + (first[2 * k :] + second[k:] + third))


def turn_kernel(total, rows_ref, sums_ref, cur_ref, image_ref, tiles_ref, next_ref, y_ref, out_ref, centre_ref, *scratch):
    cur, image, begun, block, tiles, slots, loads, sems = scratch
    first = begin(cur_ref, cur, loads.at[CHUNKS])
    second = begin(image_ref, image, loads.at[CHUNKS + 1])
    coming = load(tiles_ref, tiles, loads)
    gram, product = unpacked(sums_ref[...])
    inverse = inverse_factor(gram / total)
    half = jnp.dot(inverse, product / total, precision=HI, preferred_element_type=F32)
    centre = jnp.sum(half * inverse) / inverse.shape[0] - 1.0
    centre_ref[0, 0] = centre
    stack = jnp.concatenate(thirds(inverse), axis=0)
    first.wait()
    second.wait()
    for r in range(cur.shape[0]):
        value = apply_square(stack, cur[r]).astype(BF16)
        begun[r] = value
        turned = apply_wide(stack, image[r])
        block[r] = (turned - centre * value.astype(F32)).astype(BF16)
    going = [begin(begun, next_ref, sems.at[WAVES]), begin(block, y_ref, sems.at[WAVES + 1])]
    going += send(rows_ref, block, tiles, coming, slots, out_ref, sems)
    for copy in going:
        copy.wait()


def end_kernel(total, sums_ref, cur_ref, basis_ref, ritz_ref, cur, basis, sems):
    coming = begin(cur_ref, cur, sems.at[0])
    width = cur.shape[2]
    gram, product = unpacked(sums_ref[...])
    inverse = inverse_factor(gram / total)
    stack = jnp.concatenate(thirds(inverse), axis=0)
    coming.wait()
    for r in range(cur.shape[0]):
        basis[:, r * width : (r + 1) * width] = apply_square(stack, cur[r]).astype(BF16)
    going = begin(basis, basis_ref, sems.at[1])
    half = jnp.dot(inverse, product / total, precision=HI, preferred_element_type=F32)
    ritz_ref[...] = mm_t(half, inverse, HI)
    going.wait()


def local(vectors, diag_tiles, pair_tiles, halo_tiles, halo_rows, pair_index, pair_count):
    k, own_rows = vectors.shape
    blocks, size, _ = diag_tiles.shape
    edges, peers = pair_index.shape[1], halo_rows.shape[1]
    total = float(own_rows * peers)
    index = ((pair_index[0, :, 0], "s"), (pair_index[0, :, 1], "s"), (pair_count, "s"))
    block, spots, square = (blocks, k, size), (peers, k, size), (k, k)
    pair_tiles = pair_tiles.reshape(edges, 2, size, size)
    unit = 2 * k * size * size

    def room(shape, dtype):
        return pltpu.VMEM(shape, dtype)

    loads, sems = pltpu.SemaphoreType.DMA((CHUNKS + 2,)), pltpu.SemaphoreType.DMA((WAVES + 2,))

    def exchange(out):
        return lax.all_to_all(out, "dom", 0, 0, tiled=True)

    def own(mode, cur, extra=(), ahead=()):
        ins = [*index, *ahead, (cur, "h"), (diag_tiles, "h"), (pair_tiles, "h"), *extra]
        [part] = call(functools.partial(local_kernel, mode), [(block, F32, "h")], ins, unit * (blocks + 2 * edges), 9 << 20)
        return part

    def halo(factor, arrived, part):
        return call(
            functools.partial(halo_kernel, factor),
            [(block, BF16, "a"), (spots, BF16, "a")],
            [(halo_rows, "s"), (arrived, "v"), (halo_tiles, "a"), (part, "a")],
            unit * peers,
            10 << 20,
            [room(halo_tiles.shape, BF16), room(block, F32), room(block, F32), room(block, BF16), room(spots, BF16), loads, sems],
        )

    def everywhere(x):
        near = [list(range(g, g + NODE)) for g in range(0, peers, NODE)]
        far = [list(range(g, peers, NODE)) for g in range(NODE)]
        for groups in (near, far):
            many = jnp.broadcast_to(x[None], (len(groups[0]), *x.shape))
            x = jnp.sum(lax.all_to_all(many, "dom", 0, 0, axis_index_groups=groups, tiled=True), axis=0)
        return x

    def sums(cur, arrived, part, keep):
        [gram] = call(gram_kernel, [(square, F32, "h")], [(cur, "h")], 2 * k * k * own_rows, 1 << 20)
        outs = [(block, F32, "a")] * keep + [((k // 2 + 8, 2 * k), F32, "h")]
        ins = [(halo_rows, "s"), (arrived, "v"), (part, "a"), (cur, "a"), (gram, "h")]
        scratch = [room(block, F32), room(block, F32), room(block, BF16), sems]
        *image, value = call(functools.partial(sums_kernel, keep), outs, ins, unit * peers, 10 << 20, scratch)
        return *image, everywhere(value)

    def filtered(prev, cur, out, centre):
        for _ in range(3):
            arrived = exchange(out)
            part = own("filter", cur, [(prev, "h")], [(centre, "s")])
            prev, (cur, out) = cur, halo(2.0, arrived, part)
        return cur, out

    start, out = call(
        start_kernel,
        [(block, BF16, "a"), (spots, BF16, "a")],
        [(halo_rows, "a"), (vectors, "a"), (halo_tiles, "a")],
        unit * peers,
        8 << 20,
        [pltpu.SMEM(halo_rows.shape, jnp.int32), room(halo_tiles.shape, BF16), room(vectors.shape, BF16)]
        + [room(block, BF16), room(spots, BF16), loads, sems],
    )
    arrived = exchange(out)
    cur, out = halo(1.0, arrived, own("start", start))
    cur, out = filtered(start, cur, out, jnp.full((1, 1), FIRST_CENTRE, F32))

    arrived = exchange(out)
    image, value = sums(cur, arrived, own("image", cur), 1)
    begun, cur, out, centre = call(
        functools.partial(turn_kernel, total),
        [(block, BF16, "a"), (block, BF16, "a"), (spots, BF16, "a"), ((1, 1), F32, "s")],
        [(halo_rows, "s"), (value, "h"), (cur, "a"), (image, "a"), (halo_tiles, "a")],
        1 << 24,
        4 << 20,
        [room(block, BF16), room(block, F32), room(block, BF16), room(block, BF16)]
        + [room(halo_tiles.shape, BF16), room(spots, BF16), loads, sems],
    )
    cur, out = filtered(begun, cur, out, centre)

    arrived = exchange(out)
    [value] = sums(cur, arrived, own("image", cur), 0)
    return call(
        functools.partial(end_kernel, total),
        [((k, own_rows), BF16, "a"), (square, F32, "h")],
        [(value, "h"), (cur, "a")],
        1 << 24,
        2 << 20,
        [room(block, BF16), room(vectors.shape, BF16), sems],
    )


def solution(mesh):
    return jax.shard_map(
        local,
        mesh=mesh,
        in_specs=(
            P(None, "dom"),
            P("dom", None, None),
            P("dom", None, None, None),
            P("dom", None, None),
            P("dom", None),
            P("dom", None, None),
            P("dom"),
        ),
        out_specs=(P(None, "dom"), P()),
        check_vma=False,
    )
```

```python
import functools

import jax
import jax.numpy as jnp
from jax import lax
from jax.experimental import pallas as pl
from jax.experimental.pallas import tpu as pltpu
from jax.sharding import PartitionSpec as P

FIRST_CENTRE = -0.5
F32, BF16 = jnp.float32, jnp.bfloat16
HI = lax.Precision.HIGHEST
VM = pl.BlockSpec(memory_space=pltpu.VMEM)
SM = pl.BlockSpec(memory_space=pltpu.SMEM)


HBM = pl.BlockSpec(memory_space=pltpu.HBM)
NODE = 8
CHUNKS, WAVES = 8, 4


def call(body, outs, ins, flops, moved, scratch=()):
    place = {"a": pltpu.HBM, "v": pltpu.VMEM}
    spec = {"a": HBM, "v": VM, "h": VM, "s": SM}
    return pl.pallas_call(
        body,
        out_shape=[(place[kind] if kind in place else jax.ShapeDtypeStruct)(shape, dtype) for shape, dtype, kind in outs],
        in_specs=[spec[kind] for _, kind in ins],
        out_specs=[spec[kind] for _, _, kind in outs],
        scratch_shapes=list(scratch),
        cost_estimate=pl.CostEstimate(flops=flops, bytes_accessed=moved, transcendentals=0),
        compiler_params=pltpu.CompilerParams(vmem_limit_bytes=30 << 20),
    )(*[pltpu.with_memory_space_constraint(x, place[kind]) if kind in place else x for x, kind in ins])


def mm(a, b):
    return jnp.dot(a, b, preferred_element_type=F32)


def mm_t(a, b, precision=None):
    return lax.dot_general(a, b, (((1,), (1,)), ((), ())), precision=precision, preferred_element_type=F32)


def thirds(x):
    high = x.astype(BF16)
    rest = x - high.astype(F32)
    middle = rest.astype(BF16)
    return high, middle, (rest - middle.astype(F32)).astype(BF16)


def begin(source, target, sem):
    copy = pltpu.make_async_copy(source, target, sem)
    copy.start()
    return copy


def load(tiles_ref, tiles, sems):
    some = tiles.shape[0] // CHUNKS
    return [begin(tiles_ref.at[pl.ds(g * some, some)], tiles.at[pl.ds(g * some, some)], sems.at[g]) for g in range(CHUNKS)]


def send(rows_ref, blocks, tiles, coming, slots, out_ref, sems):
    some, ready = slots.shape[0] // WAVES, CHUNKS // WAVES
    copies = []
    for g in range(WAVES):
        for copy in coming[g * ready : (g + 1) * ready]:
            copy.wait()
        for p in range(g * some, (g + 1) * some):
            slots[p] = mm(blocks[rows_ref[0, p]], tiles[p]).astype(BF16)
        copies.append(begin(slots.at[pl.ds(g * some, some)], out_ref.at[pl.ds(g * some, some)], sems.at[g]))
    return copies


def receive(rows_ref, arrived_ref, acc):
    acc[...] = jnp.zeros(acc.shape, F32)
    for p in range(arrived_ref.shape[0]):
        acc[rows_ref[0, p]] += arrived_ref[p].astype(F32)


def start_kernel(rows_ref, vec_ref, tiles_ref, cur_ref, out_ref, rows, tiles, vec, block, slots, loads, sems):
    first = begin(vec_ref, vec, loads.at[CHUNKS])
    also = begin(rows_ref, rows, loads.at[CHUNKS + 1])
    coming = load(tiles_ref, tiles, loads)
    first.wait()
    width = block.shape[2]
    for r in range(block.shape[0]):
        block[r] = vec[:, r * width : (r + 1) * width]
    also.wait()
    going = [begin(block, cur_ref, loads.at[CHUNKS + 1])]
    going += send(rows, block, tiles, coming, slots, out_ref, sems)
    for copy in going:
        copy.wait()


def local_kernel(mode, first_ref, second_ref, count_ref, *refs):
    if mode == "filter":
        centre_ref, cur_ref, diag_ref, pair_ref, prev_ref, acc_ref = refs
        centre = centre_ref[0, 0]
    else:
        cur_ref, diag_ref, pair_ref, acc_ref = refs
        centre = FIRST_CENTRE

    def own(r, _):
        block = cur_ref[r]
        value = mm(block, diag_ref[r])
        if mode != "image":
            value = value - centre * block.astype(F32)
        if mode == "filter":
            value = value - 0.5 * prev_ref[r].astype(F32)
        acc_ref[r] = value
        return _

    lax.fori_loop(0, cur_ref.shape[0], own, 0, unroll=4)
    count = count_ref[0]
    group = 4

    def step(i, _):
        parts = []
        for u in range(group):
            e = i * group + u
            live = jnp.where(e < count, 1.0, 0.0).astype(F32)
            r, c = first_ref[e], second_ref[e]
            parts.append((r, mm(cur_ref[c], pair_ref[e, 1]) * live))
            parts.append((c, mm(cur_ref[r], pair_ref[e, 0]) * live))
        for at, value in parts:
            acc_ref[at] += value
        return _

    lax.fori_loop(0, lax.div(count + (group - 1), group), step, 0)


def halo_kernel(factor, rows_ref, arrived_ref, tiles_ref, part_ref, cur_ref, out_ref, tiles, part, acc, block, slots, loads, sems):
    also = begin(part_ref, part, loads.at[CHUNKS])
    coming = load(tiles_ref, tiles, loads)
    receive(rows_ref, arrived_ref, acc)
    also.wait()
    block[...] = (factor * (acc[...] + part[...])).astype(BF16)
    going = [begin(block, cur_ref, loads.at[CHUNKS + 1])]
    going += send(rows_ref, block, tiles, coming, slots, out_ref, sems)
    for copy in going:
        copy.wait()


def gram_kernel(cur_ref, gram_ref):
    value = jnp.zeros(gram_ref.shape, F32)
    for r in range(cur_ref.shape[0]):
        block = cur_ref[r]
        value = value + mm_t(block, block)
    gram_ref[...] = value


def corner(n):
    return lax.broadcasted_iota(jnp.int32, (n, n), 0), lax.broadcasted_iota(jnp.int32, (n, n), 1)


def packed(gram, product):
    n = gram.shape[0]
    row, col = corner(n)
    both = jnp.where(col >= row, gram, product)
    diagonal = jnp.sum(jnp.where(row == col, product, 0.0), axis=0, keepdims=True)
    last = jnp.concatenate([diagonal, jnp.zeros((1, n), F32)], axis=1)
    top = jnp.concatenate([both[: n // 2], both[n // 2 :]], axis=1)
    return jnp.concatenate([top, jnp.broadcast_to(last, (8, 2 * n))], axis=0)


def unpacked(sums):
    n = sums.shape[1] // 2
    row, col = corner(n)
    both = jnp.concatenate([sums[: n // 2, :n], sums[: n // 2, n:]], axis=0)
    turned = both.T
    diagonal = sums[n // 2 : n // 2 + 1, :n]
    gram = jnp.where(col >= row, both, turned)
    product = jnp.where(col < row, both, jnp.where(row == col, jnp.broadcast_to(diagonal, (n, n)), turned))
    return gram, product


def sums_kernel(keep, rows_ref, arrived_ref, part_ref, cur_ref, gram_ref, *refs):
    if keep:
        image_ref, sums_ref, part, acc, cur, sems = refs
    else:
        sums_ref, part, acc, cur, sems = refs
    also = begin(part_ref, part, sems.at[0])
    more = begin(cur_ref, cur, sems.at[1])
    receive(rows_ref, arrived_ref, acc)
    also.wait()
    acc[...] += part[...]
    if keep:
        going = begin(acc, image_ref, sems.at[2])
    more.wait()
    k = gram_ref.shape[0]
    value = jnp.zeros((3 * k, k), F32)
    for r in range(acc.shape[0]):
        value = value + mm_t(jnp.concatenate(thirds(acc[r]), axis=0), cur[r])
    sums_ref[...] = packed(gram_ref[...], value[:k] + (value[k : 2 * k] + value[2 * k :]))
    if keep:
        going.wait()


def inverse_factor(gram):
    n, some = gram.shape[0], 8
    row, col = corner(n)
    work = jnp.concatenate([gram, jnp.where(row == col, 1.0, 0.0).astype(F32)], axis=1)
    parts = [work[b : b + some] for b in range(0, n, some)]
    at = lax.broadcasted_iota(jnp.int32, parts[0].shape, 0)
    for own in range(len(parts)):
        live = parts[own:]
        columns = [[jnp.broadcast_to(part[:, own * some + g : own * some + g + 1], part.shape) for part in live] for g in range(some)]
        pivot = [[columns[h][0][g : g + 1] for h in range(some)] for g in range(some)]
        rows = [live[0][g : g + 1] for g in range(some)]
        over = []
        for g in range(some):
            over.append(1.0 / pivot[g][g])
            for h in range(g + 1, some):
                low = pivot[h][g] * over[g]
                rows[h] = rows[h] - low * rows[g]
                for x in range(g + 1, some):
                    pivot[h][x] = pivot[h][x] - low * pivot[g][x]
        for i, part in enumerate(live):
            times = []
            for g in range(some):
                value = columns[g][i]
                for h in range(g):
                    value = value - times[h] * pivot[h][g]
                times.append(value * over[g])
            for g in range(some):
                part = part - (jnp.where(at > g, times[g], 0.0) if i == 0 else times[g]) * rows[g]
            parts[own + i] = part
    work = jnp.concatenate(parts, axis=0)
    pivots = jnp.sum(jnp.where(row == col, work[:, :n], 0.0), axis=1, keepdims=True)
    return work[:, n:] / jnp.sqrt(pivots)


def apply_square(stack, block):
    k = stack.shape[1]
    value = mm(stack, block)
    return value[:k] + (value[k : 2 * k] + value[2 * k :])


def apply_wide(stack, block):
    k = stack.shape[1]
    high, middle, low = thirds(block)
    first, second, third = mm(stack, high), mm(stack[: 2 * k], middle), mm(stack[:k], low)
    return first[:k] + ((first[k : 2 * k] + second[:k]) + (first[2 * k :] + second[k:] + third))


def turn_kernel(total, rows_ref, sums_ref, cur_ref, image_ref, tiles_ref, next_ref, y_ref, out_ref, centre_ref, *scratch):
    cur, image, begun, block, tiles, slots, loads, sems = scratch
    first = begin(cur_ref, cur, loads.at[CHUNKS])
    second = begin(image_ref, image, loads.at[CHUNKS + 1])
    coming = load(tiles_ref, tiles, loads)
    gram, product = unpacked(sums_ref[...])
    inverse = inverse_factor(gram / total)
    half = jnp.dot(inverse, product / total, precision=HI, preferred_element_type=F32)
    centre = jnp.sum(half * inverse) / inverse.shape[0] - 1.0
    centre_ref[0, 0] = centre
    stack = jnp.concatenate(thirds(inverse), axis=0)
    first.wait()
    second.wait()
    for r in range(cur.shape[0]):
        value = apply_square(stack, cur[r]).astype(BF16)
        begun[r] = value
        turned = apply_wide(stack, image[r])
        block[r] = (turned - centre * value.astype(F32)).astype(BF16)
    going = [begin(begun, next_ref, sems.at[WAVES]), begin(block, y_ref, sems.at[WAVES + 1])]
    going += send(rows_ref, block, tiles, coming, slots, out_ref, sems)
    for copy in going:
        copy.wait()


def end_kernel(total, sums_ref, cur_ref, basis_ref, ritz_ref, cur, basis, sems):
    coming = begin(cur_ref, cur, sems.at[0])
    width = cur.shape[2]
    gram, product = unpacked(sums_ref[...])
    inverse = inverse_factor(gram / total)
    stack = jnp.concatenate(thirds(inverse), axis=0)
    coming.wait()
    for r in range(cur.shape[0]):
        basis[:, r * width : (r + 1) * width] = apply_square(stack, cur[r]).astype(BF16)
    going = begin(basis, basis_ref, sems.at[1])
    half = jnp.dot(inverse, product / total, precision=HI, preferred_element_type=F32)
    ritz_ref[...] = mm_t(half, inverse, HI)
    going.wait()


def local(vectors, diag_tiles, pair_tiles, halo_tiles, halo_rows, pair_index, pair_count):
    k, own_rows = vectors.shape
    blocks, size, _ = diag_tiles.shape
    edges, peers = pair_index.shape[1], halo_rows.shape[1]
    total = float(own_rows * peers)
    index = ((pair_index[0, :, 0], "s"), (pair_index[0, :, 1], "s"), (pair_count, "s"))
    block, spots, square = (blocks, k, size), (peers, k, size), (k, k)
    pair_tiles = pair_tiles.reshape(edges, 2, size, size)
    unit = 2 * k * size * size

    def room(shape, dtype):
        return pltpu.VMEM(shape, dtype)

    loads, sems = pltpu.SemaphoreType.DMA((CHUNKS + 2,)), pltpu.SemaphoreType.DMA((WAVES + 2,))

    def exchange(out):
        return lax.all_to_all(out, "dom", 0, 0, tiled=True)

    def own(mode, cur, extra=(), ahead=()):
        ins = [*index, *ahead, (cur, "h"), (diag_tiles, "h"), (pair_tiles, "h"), *extra]
        [part] = call(functools.partial(local_kernel, mode), [(block, F32, "h")], ins, unit * (blocks + 2 * edges), 9 << 20)
        return part

    def halo(factor, arrived, part):
        return call(
            functools.partial(halo_kernel, factor),
            [(block, BF16, "a"), (spots, BF16, "a")],
            [(halo_rows, "s"), (arrived, "v"), (halo_tiles, "a"), (part, "a")],
            unit * peers,
            10 << 20,
            [room(halo_tiles.shape, BF16), room(block, F32), room(block, F32), room(block, BF16), room(spots, BF16), loads, sems],
        )

    def everywhere(x):
        near = [list(range(g, g + NODE)) for g in range(0, peers, NODE)]
        far = [list(range(g, peers, NODE)) for g in range(NODE)]
        for groups in (near, far):
            many = jnp.broadcast_to(x[None], (len(groups[0]), *x.shape))
            x = jnp.sum(lax.all_to_all(many, "dom", 0, 0, axis_index_groups=groups, tiled=True), axis=0)
        return x

    def sums(cur, arrived, part, keep):
        [gram] = call(gram_kernel, [(square, F32, "h")], [(cur, "h")], 2 * k * k * own_rows, 1 << 20)
        outs = [(block, F32, "a")] * keep + [((k // 2 + 8, 2 * k), F32, "h")]
        ins = [(halo_rows, "s"), (arrived, "v"), (part, "a"), (cur, "a"), (gram, "h")]
        scratch = [room(block, F32), room(block, F32), room(block, BF16), sems]
        *image, value = call(functools.partial(sums_kernel, keep), outs, ins, unit * peers, 10 << 20, scratch)
        return *image, everywhere(value)

    def filtered(prev, cur, out, centre):
        for _ in range(3):
            arrived = exchange(out)
            part = own("filter", cur, [(prev, "h")], [(centre, "s")])
            prev, (cur, out) = cur, halo(2.0, arrived, part)
        return cur, out

    start, out = call(
        start_kernel,
        [(block, BF16, "a"), (spots, BF16, "a")],
        [(halo_rows, "a"), (vectors, "a"), (halo_tiles, "a")],
        unit * peers,
        8 << 20,
        [pltpu.SMEM(halo_rows.shape, jnp.int32), room(halo_tiles.shape, BF16), room(vectors.shape, BF16)]
        + [room(block, BF16), room(spots, BF16), loads, sems],
    )
    arrived = exchange(out)
    cur, out = halo(1.0, arrived, own("start", start))
    cur, out = filtered(start, cur, out, jnp.full((1, 1), FIRST_CENTRE, F32))

    arrived = exchange(out)
    image, value = sums(cur, arrived, own("image", cur), 1)
    begun, cur, out, centre = call(
        functools.partial(turn_kernel, total),
        [(block, BF16, "a"), (block, BF16, "a"), (spots, BF16, "a"), ((1, 1), F32, "s")],
        [(halo_rows, "s"), (value, "h"), (cur, "a"), (image, "a"), (halo_tiles, "a")],
        1 << 24,
        4 << 20,
        [room(block, BF16), room(block, F32), room(block, BF16), room(block, BF16)]
        + [room(halo_tiles.shape, BF16), room(spots, BF16), loads, sems],
    )
    cur, out = filtered(begun, cur, out, centre)

    arrived = exchange(out)
    _, value = sums(cur, arrived, own("image", cur), 1)
    return call(
        functools.partial(end_kernel, total),
        [((k, own_rows), BF16, "a"), (square, F32, "h")],
        [(value, "h"), (cur, "a")],
        1 << 24,
        2 << 20,
        [room(block, BF16), room(vectors.shape, BF16), sems],
    )


def solution(mesh):
    return jax.shard_map(
        local,
        mesh=mesh,
        in_specs=(
            P(None, "dom"),
            P("dom", None, None),
            P("dom", None, None, None),
            P("dom", None, None),
            P("dom", None),
            P("dom", None, None),
            P("dom"),
        ),
        out_specs=(P(None, "dom"), P()),
        check_vma=False,
    )
```
